512 devices in a mesh: tm: 64 (over x, y, core), space: 8 (over z).
Axes of the slice: x: 4, y: 8, z: 8, core: 2. Of those that a mesh axis runs over, the one named last changes fastest.
Arguments:
- frames_feat: bfloat16 [64, 16, 64, 256], P('tm', 'space'), may hold values from -16 to 16
- prompt_labels: int32 [16, 64], P('space'), may hold values from 0 to 3
- label_table: float32 [4, 256], replicated, may hold values from -6 to 6
- enc_qkv: bfloat16 [256, 768], replicated, may hold values from -0.375 to 0.375
- enc_out: bfloat16 [256, 256], replicated, may hold values from -0.375 to 0.375
- norm_gain: float32 [256], replicated, may hold values from 0.25 to 1.75
- key_proj: bfloat16 [256, 1024], replicated, may hold values from -0.375 to 0.375
- value_proj: bfloat16 [256, 1024], replicated, may hold values from -0.375 to 0.375
- read_proj: bfloat16 [1024, 256], replicated, may hold values from -0.1875 to 0.1875
- decay: float32 [64, 8], P('tm'), may hold values from 0.1 to 1
- dec_conv: bfloat16 [3, 3, 256, 64], replicated, may hold values from -0.125 to 0.125
- dec_up: bfloat16 [64, 16], replicated, may hold values from -0.75 to 0.75
Outputs:
- mask_logits: float32 [64, 64, 256], P('tm', 'space')
The draws below stay inside these ranges and needn't reach their ends.
All inputs are finite; a program needn't handle non-finite values.
Results may differ from the reference program's by a relative error of at most 0.011.
The reference program's roundings to bfloat16 on the way count: a program that leaves them out, or rounds other values in their place, can miss the bound.
Values may be sent and summed in bfloat16 or wider, within the bound.
A program may use at most 64 MiB of HBM per device.

```python
import math
import jax
import jax.numpy as jnp
from jax import lax

D = 256
ENC_HEADS = 8
MEMORY_HEADS = 8
KEY_FEATURES = 128
VAL_DIM = 128
DEC_CH = 64
LABELS = 4
UP = 4
GRID_W = 64
FRAME_COUNT = 64
GRID_H = 16


def draw_frames_feat(key, part):
    base_key = jax.random.fold_in(jax.random.fold_in(key, 301), 0)
    full_shape = (FRAME_COUNT, GRID_H, GRID_W, D)
    base_draw = jax.random.normal(base_key, full_shape, jnp.float32)
    values = base_draw
    return jnp.clip(values, -16.0, 16.0).astype(jnp.bfloat16)


def draw_decay(key, part):
    divided_keys = jax.random.split(jax.random.fold_in(key, 517), 6)
    head_pick = jax.random.randint(divided_keys[0], (MEMORY_HEADS,), 0, 8)
    slow_flag = head_pick >= 4
    slow_power = jax.random.uniform(divided_keys[1], (1, MEMORY_HEADS), jnp.float32, 0.05, 0.35)
    jitter = jax.random.uniform(divided_keys[2], (FRAME_COUNT, MEMORY_HEADS), jnp.float32, 0.5, 1.5)
    slow_rate = jnp.exp(math.log(0.1) * slow_power * jitter / FRAME_COUNT)
    fast_rate = jax.random.uniform(divided_keys[3], (FRAME_COUNT, MEMORY_HEADS), jnp.float32, 0.3, 0.75)
    decay_rates = jnp.where(slow_flag[None, :], slow_rate, fast_rate)
    surge_frames = jax.random.randint(divided_keys[4], (2,), 0, FRAME_COUNT)
    surge_mask = jnp.any(jnp.arange(FRAME_COUNT)[:, None] == surge_frames[None, :], axis=1)
    surge_multiplier = jax.random.uniform(divided_keys[5], (FRAME_COUNT, MEMORY_HEADS), jnp.float32, 0.55, 0.8)
    decay_rates = jnp.where(surge_mask[:, None], decay_rates * surge_multiplier, decay_rates)
    return jnp.clip(decay_rates, 0.1, 1.0).astype(jnp.float32)


def place_ends(result, own_key, low, largest):
    dims = result.shape
    spot = [jax.random.randint(jax.random.fold_in(own_key, axis), (), 0, dims[axis]) for axis in range(len(dims))]
    result = result.at[tuple(spot)].set(low)
    longest = dims.index(max(dims))
    spot[longest] = (spot[longest] + 1) % dims[longest]
    return result.at[tuple(spot)].set(largest)


def centred(key, extent, deviation, limit, held_as=jnp.bfloat16):
    array = jax.random.normal(key, extent, jnp.float32) * deviation
    return jnp.minimum(jnp.maximum(array, -limit), limit).astype(held_as)


def setup_inputs(seed: int = 0) -> dict:
    key_list = jax.random.split(jax.random.key(seed), 13)
    frames_feat = draw_frames_feat(jax.random.fold_in(key_list[12], 71), 0)
    prompt_labels = place_ends(jax.random.randint(key_list[1], (GRID_H, GRID_W), 0, LABELS), jax.random.fold_in(key_list[1], 1), 0, LABELS - 1).astype(jnp.int32)
    label_table = centred(key_list[2], (LABELS, D), 1.0, 6.0, jnp.float32)
    enc_qkv = centred(key_list[3], (D, 3 * D), D ** -0.5, 0.375)
    enc_out = centred(key_list[4], (D, D), D ** -0.5, 0.375)
    norm_gain = jnp.clip(1.0 + 0.15 * jax.random.normal(key_list[5], (D,), jnp.float32), 0.25, 1.75)
    key_proj = centred(key_list[6], (D, MEMORY_HEADS * KEY_FEATURES), D ** -0.5, 0.375)
    value_proj = centred(key_list[7], (D, MEMORY_HEADS * VAL_DIM), D ** -0.5, 0.375)
    read_proj = centred(key_list[8], (MEMORY_HEADS * VAL_DIM, D), (MEMORY_HEADS * VAL_DIM) ** -0.5, 0.1875)
    decay = draw_decay(jax.random.fold_in(key_list[12], 71), 0)
    dec_conv = centred(key_list[10], (3, 3, D, DEC_CH), (9 * D) ** -0.5, 0.125)
    dec_up = centred(key_list[11], (DEC_CH, UP * UP), DEC_CH ** -0.5, 0.75)
    return dict(frames_feat=frames_feat, prompt_labels=prompt_labels, label_table=label_table, enc_qkv=enc_qkv, enc_out=enc_out, norm_gain=norm_gain, key_proj=key_proj, value_proj=value_proj, read_proj=read_proj, decay=decay, dec_conv=dec_conv, dec_up=dec_up)


epsilon = 1e-06
precise_result = lax.Precision.HIGHEST

def pool_pairs(features):
    frame_count, height, breadth, channels = features.shape
    grouped = features.astype(jnp.float32).reshape(frame_count, height // 2, 2, breadth // 2, 2, channels)
    return lax.optimization_barrier(jnp.mean(grouped, axis=(2, 4))).astype(jnp.bfloat16)

def gain_norm(hidden, gain_row):
    return hidden * lax.rsqrt(lax.optimization_barrier(jnp.mean(hidden * hidden, axis=-1, keepdims=True)) + epsilon) * gain_row

def reference(frames_feat, prompt_labels, label_table, enc_qkv, enc_out, norm_gain, key_proj, value_proj, read_proj, decay, dec_conv, dec_up):
    head_size = D // ENC_HEADS
    frame_tokens = GRID_H * GRID_W
    flat_rows = frames_feat.reshape(FRAME_COUNT, frame_tokens, D)
    pooled = pool_pairs(frames_feat).reshape(FRAME_COUNT, frame_tokens // 4, D)

    def encode_frame(inputs):
        tok_rows, pooled_rows = inputs
        queries = jnp.dot(tok_rows, enc_qkv[:, :D], preferred_element_type=jnp.float32).astype(jnp.bfloat16)
        pair_kv = jnp.dot(pooled_rows, enc_qkv[:, D:], preferred_element_type=jnp.float32).astype(jnp.bfloat16)
        query_heads = queries.astype(jnp.float32).reshape(frame_tokens, ENC_HEADS, head_size)
        key_head_rows = pair_kv[:, :D].astype(jnp.float32).reshape(-1, ENC_HEADS, head_size)
        value_head_rows = pair_kv[:, D:].astype(jnp.float32).reshape(-1, ENC_HEADS, head_size)
        scores = jnp.einsum('tha,nha->htn', query_heads, key_head_rows, precision=precise_result) * head_size ** (-0.5)
        weights = jnp.exp(scores - lax.optimization_barrier(jnp.max(scores, axis=-1, keepdims=True)))
        totals = lax.optimization_barrier(jnp.sum(weights, axis=-1))
        rounded = lax.optimization_barrier(weights.astype(jnp.bfloat16)).astype(jnp.float32)
        attended = jnp.einsum('htn,nha->hta', rounded, value_head_rows, precision=precise_result) / totals[..., None]
        attended = attended.transpose(1, 0, 2).reshape(frame_tokens, D).astype(jnp.bfloat16)
        hidden = tok_rows.astype(jnp.float32) + jnp.dot(attended, enc_out, preferred_element_type=jnp.float32)
        return gain_norm(hidden, norm_gain).astype(jnp.bfloat16)
    encoded = lax.map(encode_frame, (flat_rows, pooled))
    label_rows = label_table[prompt_labels.reshape(frame_tokens)]
    first_flag = (jnp.arange(FRAME_COUNT) == 0).astype(jnp.float32)

    def frame_state(inputs):
        encoded_rows, flag_value = inputs
        key_rows = jnp.dot(encoded_rows, key_proj, preferred_element_type=jnp.float32).astype(jnp.bfloat16)
        memory_in = (encoded_rows.astype(jnp.float32) + flag_value * label_rows).astype(jnp.bfloat16)
        value_rows = jnp.dot(memory_in, value_proj, preferred_element_type=jnp.float32).astype(jnp.bfloat16)
        key_head_rows = key_rows.astype(jnp.float32).reshape(frame_tokens, MEMORY_HEADS, KEY_FEATURES)
        value_head_rows = value_rows.astype(jnp.float32).reshape(frame_tokens, MEMORY_HEADS, VAL_DIM)
        cleared_state = jnp.einsum('gmp,gmz->mpz', key_head_rows, value_head_rows, precision=precise_result) * frame_tokens ** (-0.5)
        return (key_rows, cleared_state)
    key_rows, states = lax.map(frame_state, (encoded, first_flag))

    def advance(carried, inputs):
        rate_row, cleared_state = inputs
        memory = rate_row[:, None, None] * carried
        return (memory + cleared_state, memory)
    zero_state = jnp.zeros((MEMORY_HEADS, KEY_FEATURES, VAL_DIM), jnp.float32)
    _, memory = lax.scan(advance, zero_state, (decay, states))

    def read_frame(inputs):
        frame_keys, encoded_rows, memory_now = inputs
        truncated_memory = lax.optimization_barrier(memory_now.astype(jnp.bfloat16)).astype(jnp.float32)
        key_head_rows = frame_keys.astype(jnp.float32).reshape(frame_tokens, MEMORY_HEADS, KEY_FEATURES)
        memory_output = jnp.einsum('gba,ban->gbn', key_head_rows, truncated_memory, precision=precise_result) * KEY_FEATURES ** (-0.5)
        memory_output = memory_output.reshape(frame_tokens, MEMORY_HEADS * VAL_DIM).astype(jnp.bfloat16)
        joined_rows = encoded_rows.astype(jnp.float32) + jnp.dot(memory_output, read_proj, preferred_element_type=jnp.float32)
        return joined_rows.astype(jnp.bfloat16)
    decoder_in = lax.map(read_frame, (key_rows, encoded, memory)).reshape(FRAME_COUNT, GRID_H, GRID_W, D)

    def decode_frame(plane_rows):
        padded = jnp.pad(plane_rows, ((1, 1), (1, 1), (0, 0)))
        convolved = jnp.zeros((GRID_H * GRID_W, DEC_CH), jnp.float32)
        for row_shift in range(3):
            for col_shift in range(3):
                window = padded[row_shift:row_shift + GRID_H, col_shift:col_shift + GRID_W, :].reshape(GRID_H * GRID_W, D)
                convolved = convolved + jnp.dot(window, dec_conv[row_shift, col_shift], preferred_element_type=jnp.float32)
        mapped = jax.nn.gelu(convolved).astype(jnp.bfloat16)
        pixels = jnp.dot(mapped, dec_up, preferred_element_type=jnp.float32).reshape(GRID_H, GRID_W, UP, UP)
        return pixels.transpose(0, 2, 1, 3).reshape(GRID_H * UP, GRID_W * UP)
    return lax.map(decode_frame, decoder_in)
```

```python
import math

import jax
import jax.numpy as jnp
from jax import lax
from jax.experimental import pallas as pl
from jax.experimental.pallas import tpu as pltpu
from jax.sharding import PartitionSpec as P

MESH = pl.DeviceIdType.MESH
BF16 = jnp.bfloat16
F32 = jnp.float32

FRAMES = 64
BANDS = 8
OWNERS = 16
STRIDE = FRAMES // OWNERS
TOK = 128
DIM = 256
HEADS = 8
HEAD = DIM // HEADS
FEAT = 128
CH = 64
TAPS = 9
FAR_FIRST = (4, 3, 5, 2, 6, 1, 7)


def mm(a, b):
    return jnp.dot(a, b, preferred_element_type=F32)


def mm_nt(a, b):
    return lax.dot_general(a, b, (((1,), (1,)), ((), ())), preferred_element_type=F32)


def turned(x):
    return x.astype(F32).T.astype(x.dtype)


def iota(shape, dim):
    return lax.broadcasted_iota(jnp.int32, shape, dim)


def three_parts(x):
    high = x.astype(BF16)
    rest = x - high.astype(F32)
    middle = rest.astype(BF16)
    low = (rest - middle.astype(F32)).astype(BF16)
    return high, middle, low


def kernel(
    frames, labels, table, qkv, eo, gain, kp, vp, rp, decay, conv, up,
    out,
    x_v, lab_v, tab_v, qkv_v, eo_v, gain_v, kp_v, vp_v, rp_v, dec_v, conv_v, up_v,
    wq_t, eo_t, kp_t, vp_t, tab_t, gain_b, taps_t, up_x, spread,
    pool, hot, xt, kmask, v_t, e_t, e_tmp, k_t,
    state, states, decays, decay_own, memories, memory,
    conved, part, parts,
    load, send, pool_in, hot_in, xt_in, decay_in, state_in, memory_in, part_in,
):
    tm, sp = lax.axis_index("tm"), lax.axis_index("space")
    is_owner = lax.rem(tm, STRIDE) == 0

    barrier = pltpu.get_barrier_semaphore()
    for k in range(1, BANDS):
        pl.semaphore_signal(
            barrier, inc=1, device_id=(tm, lax.rem(sp + k, BANDS)), device_id_type=MESH
        )

    @pl.when(is_owner)
    def _():
        @pl.loop(1, FRAMES)
        def _(k):
            pl.semaphore_signal(
                barrier, inc=1, device_id=(lax.rem(tm + k, FRAMES), sp), device_id_type=MESH
            )

    @pl.when(jnp.logical_not(is_owner))
    def _():
        @pl.loop(0, OWNERS)
        def _(k):
            pl.semaphore_signal(barrier, inc=1, device_id=(k * STRIDE, sp), device_id_type=MESH)

    col = pl.multiple_of(sp * FEAT, FEAT)
    loads = [
        (frames.at[0], x_v),
        (labels, lab_v),
        (decay, dec_v),
        (qkv, qkv_v),
        (table, tab_v),
        (eo, eo_v),
        (gain, gain_v),
        (kp.at[:, pl.ds(col, FEAT)], kp_v),
        (vp.at[:, pl.ds(col, FEAT)], vp_v),
        (rp.at[pl.ds(col, FEAT), :], rp_v),
        (conv, conv_v),
        (up, up_v),
    ]
    loads = [pltpu.make_async_copy(s, d, load.at[n]) for n, (s, d) in enumerate(loads)]
    for c in loads:
        c.start()

    loads[0].wait()
    x = x_v[...].reshape(TOK, DIM)
    pr, pc = iota((TOK // 4, TOK), 0), iota((TOK // 4, TOK), 1)
    quarter = jnp.where(lax.rem(pc, 64) // 2 == pr, 0.25, 0.0).astype(BF16)
    pool[sp] = mm(quarter, x).astype(BF16)
    loads[1].wait()
    lab = lab_v[...]
    lab_row = jnp.concatenate([lab[0:1], lab[1:2]], axis=1)
    hit = (jnp.broadcast_to(lab_row, (16, TOK)) == iota((16, TOK), 0)) & (tm == 0)
    hot[sp] = jnp.where(hit, 1.0, 0.0).astype(BF16)
    loads[2].wait()
    rate = jnp.sum(
        jnp.where(iota((1, HEADS), 1) == sp, dec_v[...], 0.0), axis=1, keepdims=True
    )
    decay_own[...] = jnp.broadcast_to(rate, (8, FEAT))

    @pl.when(is_owner)
    def _():
        pl.semaphore_wait(barrier, BANDS - 1 + FRAMES - 1)

    @pl.when(jnp.logical_not(is_owner))
    def _():
        pl.semaphore_wait(barrier, BANDS - 1 + OWNERS)

    def to_band(k, buf, n, sem):
        pltpu.make_async_remote_copy(
            src_ref=buf.at[sp],
            dst_ref=buf.at[sp],
            send_sem=send.at[n],
            recv_sem=sem,
            device_id=(tm, lax.rem(sp + k, BANDS)),
            device_id_type=MESH,
        ).start()

    def arrived(ref, sem):
        pltpu.make_async_copy(ref, ref, sem).wait()

    for k in FAR_FIRST:
        to_band(k, pool, 0, pool_in)
    xt[sp] = x.astype(F32).T.astype(BF16)
    for k in (1, 7, 2, 6, 3, 5, 4):
        to_band(k, hot, 1, hot_in)
        to_band(k, xt, 2, xt_in.at[k])

    def to_owners(src, dst, n, sem):
        for c in range(OWNERS):
            @pl.when(tm != c * STRIDE)
            def _():
                pltpu.make_async_remote_copy(
                    src_ref=src(c),
                    dst_ref=dst.at[tm],
                    send_sem=send.at[n],
                    recv_sem=sem,
                    device_id=(c * STRIDE, sp),
                    device_id_type=MESH,
                ).start()

    to_owners(lambda c: decay_own, decays, 3, decay_in)

    for c in loads[3:]:
        c.wait()
    wq_t[...] = turned(qkv_v[:, :DIM])
    eo_t[...] = turned(eo_v[...])
    kp_t[...] = turned(kp_v[...])
    vp_t[...] = turned(vp_v[...])
    tab = jnp.concatenate([tab_v[...], jnp.zeros((12, DIM), F32)], axis=0)
    tab_t[...] = turned(jnp.concatenate(three_parts(tab), axis=0))
    gain_b[...] = jnp.broadcast_to(gain_v[...], (TOK, DIM)).T

    @pl.loop(0, TAPS)
    def _(n):
        tap = conv_v[n]
        both = mm(rp_v[...], tap).T.astype(BF16)
        own = conv_v[n, pl.ds(pl.multiple_of(sp * HEAD, HEAD), HEAD), :].astype(F32).T.astype(BF16)
        taps_t[pl.ds(pl.multiple_of(n * CH, CH), CH), :] = jnp.concatenate([both, own], axis=1)

    row, src_row = iota((32, 16), 0), iota((32, 16), 1)
    picks = jnp.where(src_row == 4 * lax.rem(row, 4) + row // 8, 1.0, 0.0).astype(BF16)
    up_x[...] = mm_nt(picks, up_v[...]).astype(BF16)
    er, ec = iota((4 * TOK, DIM), 0), iota((4 * TOK, DIM), 1)
    spread[...] = jnp.where(ec == 4 * lax.rem(er, 64) + er // TOK, 1.0, 0.0).astype(BF16)

    arrived(pool.at[pl.ds(0, BANDS - 1)], pool_in)
    pooled = pool[...].reshape(BANDS * TOK // 4, DIM)
    kv = mm(pooled, qkv_v[:, DIM:])
    keys = kv[:, :DIM].astype(BF16)
    v_t[...] = kv[:, DIM:].T.astype(BF16)
    lane_head = iota((DIM, DIM), 1) // HEAD
    for h in range(HEADS):
        kmask[h] = jnp.where(lane_head == h, keys, jnp.zeros_like(keys))
    arrived(hot.at[pl.ds(0, BANDS - 1)], hot_in)

    state[...] = jnp.zeros_like(state)
    factor = HEAD**-0.5 * math.log2(math.e)

    @pl.loop(0, BANDS // 2)
    def _(p):
        k0, k1 = p, BANDS - 1 - p

        @pl.when(p > 0)
        def _():
            arrived(xt.at[0], xt_in.at[k0])

        arrived(xt.at[0], xt_in.at[k1])
        b0, b1 = lax.rem(sp + BANDS - k0, BANDS), lax.rem(sp + BANDS - k1, BANDS)
        xp = jnp.concatenate([xt[b0], xt[b1]], axis=1)
        q = mm(wq_t[...], xp).astype(BF16)
        attended = []
        for h in range(HEADS):
            s = mm(kmask[h], q)
            w = jnp.exp2((s - jnp.max(s, axis=0, keepdims=True)) * factor)
            total = jnp.sum(w, axis=0, keepdims=True)
            a = mm(v_t[h * HEAD : (h + 1) * HEAD, :], w.astype(BF16))
            attended.append((a / total).astype(BF16))
        hidden = xp.astype(F32) + mm(eo_t[...], jnp.concatenate(attended, axis=0))
        scale = lax.rsqrt(jnp.mean(hidden * hidden, axis=0, keepdims=True) + 1e-06)
        gains = jnp.concatenate([gain_b[...], gain_b[...]], axis=1)
        encoded = (hidden * scale * gains).astype(BF16)
        e_tmp[...] = encoded
        own = e_tmp[pl.ds(pl.multiple_of(sp * HEAD, HEAD), HEAD), :]
        e_t[b0] = own[:, :TOK]
        e_t[b1] = own[:, TOK:]
        key = mm(kp_t[...], encoded).astype(BF16)
        k_t[b0] = key[:, :TOK]
        k_t[b1] = key[:, TOK:]
        mark = jnp.concatenate([hot[b0], hot[b1]], axis=1)
        mark = jnp.concatenate([mark, mark, mark], axis=0)
        told = (encoded.astype(F32) + mm(tab_t[...], mark)).astype(BF16)
        value = mm(vp_t[...], told).astype(BF16)
        state[...] += mm_nt(value, key).reshape(OWNERS, 8, FEAT)

    state[...] = state[...] * (BANDS * TOK) ** -0.5

    to_owners(lambda c: state.at[c], states, 4, state_in)

    @pl.when(is_owner)
    def _():
        states[tm] = state[tm // STRIDE]
        decays[tm] = decay_own[...]
        arrived(decays.at[pl.ds(0, FRAMES - 1)], decay_in)
        arrived(states.at[pl.ds(0, FRAMES - 1)], state_in)
        place = tm // STRIDE

        def frame(t, held):
            held = decays[t] * held
            memories[t] = held

            @pl.when(t != tm)
            def _():
                pltpu.make_async_remote_copy(
                    src_ref=memories.at[t],
                    dst_ref=memory.at[place],
                    send_sem=send.at[5],
                    recv_sem=memory_in,
                    device_id=(t, sp),
                    device_id_type=MESH,
                ).start()

            return held + states[t]

        lax.fori_loop(0, FRAMES, frame, jnp.zeros((8, FEAT), F32))
        memory[place] = memories[tm]
        arrived(memory.at[pl.ds(0, OWNERS - 1)], memory_in)

    @pl.when(jnp.logical_not(is_owner))
    def _():
        arrived(memory, memory_in)

    now = memory[...].reshape(FEAT, FEAT).astype(BF16)
    for p in range(BANDS // 2):
        key = jnp.concatenate([k_t[2 * p], k_t[2 * p + 1]], axis=1)
        own = jnp.concatenate([e_t[2 * p], e_t[2 * p + 1]], axis=1)
        read = (mm(now, key) * FEAT**-0.5).astype(BF16)
        c = mm(taps_t[...], jnp.concatenate([read, own], axis=0))
        conved[2 * p] = c[:, :TOK]
        conved[2 * p + 1] = c[:, TOK:]
    lane = iota((CH, TOK), 1)
    column = lax.rem(lane, 64)

    def tap(n, a, b):
        at = (a * 3 + b) * CH
        return conved[n, at : at + CH, :]

    for n in range(BANDS):
        shifted = []
        for b in range(3):
            late, early = tap(n, 2, b), tap(n, 0, b)
            if n > 0:
                late = late + tap(n - 1, 0, b)
            if n < BANDS - 1:
                early = early + tap(n + 1, 2, b)
            shifted.append(tap(n, 1, b) + pltpu.roll(jnp.where(lane >= 64, late, early), 64, 1))
        total = shifted[1]
        total = total + jnp.where(column != 63, pltpu.roll(shifted[2], TOK - 1, 1), 0.0)
        total = total + jnp.where(column != 0, pltpu.roll(shifted[0], 1, 1), 0.0)
        part[n] = total.astype(BF16)

        @pl.when(sp != n)
        def _():
            pltpu.make_async_remote_copy(
                src_ref=part.at[n],
                dst_ref=parts.at[sp],
                send_sem=send.at[6],
                recv_sem=part_in,
                device_id=(tm, n),
                device_id_type=MESH,
            ).start()

    parts[sp] = part[sp]
    arrived(parts.at[pl.ds(0, BANDS - 1)], part_in)
    total = parts[0].astype(F32)
    for n in range(1, BANDS):
        total = total + parts[n].astype(F32)
    cubic = total + 0.044715 * (total * total * total)
    hidden = (0.5 * total * (1.0 + jnp.tanh(math.sqrt(2 / math.pi) * cubic))).astype(BF16)
    pixels = mm(up_x[...], hidden)
    keep = (lax.rem(iota((32, TOK), 0) // 4, 2)) == (iota((32, TOK), 1) // 64)
    pixels = jnp.where(keep, pixels, 0.0)
    wide = jnp.concatenate([pixels[8 * b : 8 * b + 8] for b in range(4)], axis=1)
    high, middle, low = three_parts(wide)
    high = mm(high, spread[...])
    out[0] = high + (mm(middle, spread[...]) + mm(low, spread[...]))

    arrived(pool.at[pl.ds(0, BANDS - 1)], send.at[0])
    arrived(hot.at[pl.ds(0, BANDS - 1)], send.at[1])
    arrived(xt.at[pl.ds(0, BANDS - 1)], send.at[2])

    @pl.when(is_owner)
    def _():
        arrived(state.at[pl.ds(0, OWNERS - 1)], send.at[3])
        arrived(state.at[pl.ds(0, OWNERS - 1)], send.at[4])
        arrived(memories.at[pl.ds(0, FRAMES - 1)], send.at[5])

    @pl.when(jnp.logical_not(is_owner))
    def _():
        arrived(state, send.at[3])
        arrived(state, send.at[4])

    arrived(part.at[pl.ds(0, BANDS - 1)], send.at[6])


def shards(frames, labels, table, qkv, eo, gain, kp, vp, rp, decay, conv, up):
    vmem = pltpu.VMEM
    dma = pltpu.SemaphoreType.DMA
    scratch = [
        vmem((2, 64, DIM), BF16), vmem((2, 64), jnp.int32), vmem((4, DIM), F32),
        vmem((DIM, 3 * DIM), BF16), vmem((DIM, DIM), BF16), vmem((1, DIM), F32),
        vmem((DIM, FEAT), BF16), vmem((DIM, FEAT), BF16), vmem((FEAT, DIM), BF16),
        vmem((1, HEADS), F32), vmem((TAPS, DIM, CH), BF16), vmem((CH, 16), BF16),
        vmem((DIM, DIM), BF16), vmem((DIM, DIM), BF16), vmem((FEAT, DIM), BF16),
        vmem((FEAT, DIM), BF16), vmem((DIM, 48), BF16), vmem((DIM, TOK), F32),
        vmem((TAPS * CH, FEAT + HEAD), BF16), vmem((32, CH), BF16), vmem((4 * TOK, DIM), BF16),
        vmem((BANDS, TOK // 4, DIM), BF16), vmem((BANDS, 16, TOK), BF16),
        vmem((BANDS, DIM, TOK), BF16), vmem((HEADS, DIM, DIM), BF16), vmem((DIM, DIM), BF16),
        vmem((BANDS, HEAD, TOK), BF16), vmem((DIM, 2 * TOK), BF16), vmem((BANDS, FEAT, TOK), BF16),
        vmem((OWNERS, 8, FEAT), F32), vmem((FRAMES, 8, FEAT), F32), vmem((FRAMES, 8, FEAT), F32),
        vmem((8, FEAT), F32), vmem((FRAMES, 8, FEAT), F32), vmem((OWNERS, 8, FEAT), F32),
        vmem((BANDS, TAPS * CH, TOK), F32), vmem((BANDS, CH, TOK), BF16),
        vmem((BANDS, CH, TOK), BF16),
        dma((12,)), dma((7,)), dma, dma, dma((BANDS,)), dma, dma, dma, dma,
    ]
    return pl.pallas_call(
        kernel,
        out_shape=jax.ShapeDtypeStruct((1, 8, DIM), F32),
        in_specs=[pl.BlockSpec(memory_space=pl.ANY)] * 12,
        out_specs=pl.BlockSpec(memory_space=pltpu.VMEM),
        scratch_shapes=scratch,
        compiler_params=pltpu.CompilerParams(
            collective_id=0, has_side_effects=True, vmem_limit_bytes=48 * 1024 * 1024
        ),
        name="propagate",
    )(
        frames, labels, table, qkv, eo, gain.reshape(1, DIM), kp, vp, rp, decay,
        conv.reshape(TAPS, DIM, CH), up,
    )


def solution(mesh):
    return jax.shard_map(
        shards,
        mesh=mesh,
        in_specs=(
            P("tm", "space", None, None), P("space", None), P(), P(), P(), P(), P(), P(), P(),
            P("tm", None), P(), P(),
        ),
        out_specs=P("tm", "space", None),
        check_vma=False,
    )
```

```python
import math

import jax
import jax.numpy as jnp
from jax import lax
from jax.experimental import pallas as pl
from jax.experimental.pallas import tpu as pltpu
from jax.sharding import PartitionSpec as P

MESH = pl.DeviceIdType.MESH
BF16 = jnp.bfloat16
F32 = jnp.float32

FRAMES = 64
BANDS = 8
OWNERS = 16
STRIDE = FRAMES // OWNERS
TOK = 128
DIM = 256
HEADS = 8
HEAD = DIM // HEADS
FEAT = 128
CH = 64
TAPS = 9
FAR_FIRST = (4, 3, 5, 2, 6, 1, 7)


def mm(a, b):
    return jnp.dot(a, b, preferred_element_type=F32)


def mm_nt(a, b):
    return lax.dot_general(a, b, (((1,), (1,)), ((), ())), preferred_element_type=F32)


def turned(x):
    return x.astype(F32).T.astype(x.dtype)


def iota(shape, dim):
    return lax.broadcasted_iota(jnp.int32, shape, dim)


def three_parts(x):
    high = x.astype(BF16)
    rest = x - high.astype(F32)
    middle = rest.astype(BF16)
    low = (rest - middle.astype(F32)).astype(BF16)
    return high, middle, low


def kernel(
    frames, labels, table, qkv, eo, gain, kp, vp, rp, decay, conv, up,
    out,
    x_v, lab_v, tab_v, qkv_v, eo_v, gain_v, kp_v, vp_v, rp_v, dec_v, conv_v, up_v,
    wq_t, eo_t, kp_t, vp_t, tab_t, gain_b, taps_t, up_x, spread,
    pool, hot, xt, kmask, v_mask, weights, e_t, e_tmp, k_t,
    state, states, decays, decay_own, memories, memory,
    conved, part, parts,
    load, send, pool_in, hot_in, xt_in, decay_in, state_in, memory_in, part_in,
):
    tm, sp = lax.axis_index("tm"), lax.axis_index("space")
    is_owner = lax.rem(tm, STRIDE) == 0

    barrier = pltpu.get_barrier_semaphore()
    for k in range(1, BANDS):
        pl.semaphore_signal(
            barrier, inc=1, device_id=(tm, lax.rem(sp + k, BANDS)), device_id_type=MESH
        )

    @pl.when(is_owner)
    def _():
        @pl.loop(1, FRAMES)
        def _(k):
            pl.semaphore_signal(
                barrier, inc=1, device_id=(lax.rem(tm + k, FRAMES), sp), device_id_type=MESH
            )

    @pl.when(jnp.logical_not(is_owner))
    def _():
        @pl.loop(0, OWNERS)
        def _(k):
            pl.semaphore_signal(barrier, inc=1, device_id=(k * STRIDE, sp), device_id_type=MESH)

    col = pl.multiple_of(sp * FEAT, FEAT)
    loads = [
        (frames.at[0], x_v),
        (labels, lab_v),
        (decay, dec_v),
        (qkv, qkv_v),
        (table, tab_v),
        (eo, eo_v),
        (gain, gain_v),
        (kp.at[:, pl.ds(col, FEAT)], kp_v),
        (vp.at[:, pl.ds(col, FEAT)], vp_v),
        (rp.at[pl.ds(col, FEAT), :], rp_v),
        (conv, conv_v),
        (up, up_v),
    ]
    loads = [pltpu.make_async_copy(s, d, load.at[n]) for n, (s, d) in enumerate(loads)]
    for c in loads:
        c.start()

    loads[0].wait()
    x = x_v[...].reshape(TOK, DIM)
    pr, pc = iota((TOK // 4, TOK), 0), iota((TOK // 4, TOK), 1)
    quarter = jnp.where(lax.rem(pc, 64) // 2 == pr, 0.25, 0.0).astype(BF16)
    pool[sp] = mm(quarter, x).astype(BF16)
    loads[1].wait()
    lab = lab_v[...]
    lab_row = jnp.concatenate([lab[0:1], lab[1:2]], axis=1)
    hit = (jnp.broadcast_to(lab_row, (16, TOK)) == iota((16, TOK), 0)) & (tm == 0)
    hot[sp] = jnp.where(hit, 1.0, 0.0).astype(BF16)
    loads[2].wait()
    rate = jnp.sum(
        jnp.where(iota((1, HEADS), 1) == sp, dec_v[...], 0.0), axis=1, keepdims=True
    )
    decay_own[...] = jnp.broadcast_to(rate, (8, FEAT))

    @pl.when(is_owner)
    def _():
        pl.semaphore_wait(barrier, BANDS - 1 + FRAMES - 1)

    @pl.when(jnp.logical_not(is_owner))
    def _():
        pl.semaphore_wait(barrier, BANDS - 1 + OWNERS)

    def to_band(k, buf, n, sem):
        pltpu.make_async_remote_copy(
            src_ref=buf.at[sp],
            dst_ref=buf.at[sp],
            send_sem=send.at[n],
            recv_sem=sem,
            device_id=(tm, lax.rem(sp + k, BANDS)),
            device_id_type=MESH,
        ).start()

    def arrived(ref, sem):
        pltpu.make_async_copy(ref, ref, sem).wait()

    for k in FAR_FIRST:
        to_band(k, pool, 0, pool_in)
    xt[sp] = x.astype(F32).T.astype(BF16)
    for k in (1, 7, 2, 6, 3, 5, 4):
        to_band(k, hot, 1, hot_in)
        to_band(k, xt, 2, xt_in.at[k])

    def to_owners(src, dst, n, sem):
        for c in range(OWNERS):
            @pl.when(tm != c * STRIDE)
            def _():
                pltpu.make_async_remote_copy(
                    src_ref=src(c),
                    dst_ref=dst.at[tm],
                    send_sem=send.at[n],
                    recv_sem=sem,
                    device_id=(c * STRIDE, sp),
                    device_id_type=MESH,
                ).start()

    to_owners(lambda c: decay_own, decays, 3, decay_in)

    for c in loads[3:]:
        c.wait()
    wq_t[...] = turned(qkv_v[:, :DIM])
    eo_t[...] = turned(eo_v[...])
    kp_t[...] = turned(kp_v[...])
    vp_t[...] = turned(vp_v[...])
    tab = jnp.concatenate([tab_v[...], jnp.zeros((12, DIM), F32)], axis=0)
    tab_t[...] = turned(jnp.concatenate(three_parts(tab), axis=0))
    gain_b[...] = jnp.broadcast_to(gain_v[...], (TOK, DIM)).T

    here = jnp.where(iota((DIM, HEAD), 0) == sp * HEAD + iota((DIM, HEAD), 1), 1.0, 0.0).astype(BF16)

    @pl.loop(0, TAPS)
    def _(n):
        both = mm_nt(conv_v[n], rp_v[...]).astype(BF16)
        own = mm(conv_v[n], here).astype(BF16)
        taps_t[pl.ds(pl.multiple_of(n * CH, CH), CH), :] = jnp.concatenate([both, own], axis=1)

    row, src_row = iota((32, 16), 0), iota((32, 16), 1)
    picks = jnp.where(src_row == 4 * lax.rem(row, 4) + row // 8, 1.0, 0.0).astype(BF16)
    up_x[...] = mm(picks, up_v[...]).astype(BF16)
    er, ec = iota((4 * TOK, DIM), 0), iota((4 * TOK, DIM), 1)
    spread[...] = jnp.where(ec == 4 * lax.rem(er, 64) + er // TOK, 1.0, 0.0).astype(BF16)

    arrived(pool.at[pl.ds(0, BANDS - 1)], pool_in)
    pooled = pool[...].reshape(BANDS * TOK // 4, DIM)
    kv = mm(pooled, qkv_v[:, DIM:])
    keys = kv[:, :DIM].astype(BF16)
    values = kv[:, DIM:].T.astype(BF16)
    lane_head, row_head = iota((DIM, DIM), 1) // HEAD, iota((DIM, DIM), 0) // HEAD
    for h in range(HEADS):
        kmask[h * DIM : (h + 1) * DIM, :] = jnp.where(lane_head == h, keys, jnp.zeros_like(keys))
        v_mask[:, h * DIM : (h + 1) * DIM] = jnp.where(row_head == h, values, jnp.zeros_like(values))
    arrived(hot.at[pl.ds(0, BANDS - 1)], hot_in)

    state[...] = jnp.zeros_like(state)
    factor = HEAD**-0.5 * math.log2(math.e)

    @pl.loop(0, BANDS // 2)
    def _(p):
        k0, k1 = p, BANDS - 1 - p

        @pl.when(p > 0)
        def _():
            arrived(xt.at[0], xt_in.at[k0])

        arrived(xt.at[0], xt_in.at[k1])
        b0, b1 = lax.rem(sp + BANDS - k0, BANDS), lax.rem(sp + BANDS - k1, BANDS)
        xp = jnp.concatenate([xt[b0], xt[b1]], axis=1)
        q = mm(wq_t[...], xp).astype(BF16)
        scores = mm(kmask[...], q)
        inverse = []
        for h in range(HEADS):
            s = scores[h * DIM : (h + 1) * DIM]
            w = jnp.exp2((s - jnp.max(s, axis=0, keepdims=True)) * factor)
            inverse.append(
                jnp.broadcast_to(1.0 / jnp.sum(w, axis=0, keepdims=True), (HEAD, 2 * TOK))
            )
            weights[h * DIM : (h + 1) * DIM, :] = w.astype(BF16)
        summed = mm(v_mask[...], weights[...])
        attended = (summed * jnp.concatenate(inverse, axis=0)).astype(BF16)
        hidden = xp.astype(F32) + mm(eo_t[...], attended)
        scale = lax.rsqrt(jnp.mean(hidden * hidden, axis=0, keepdims=True) + 1e-06)
        gains = jnp.concatenate([gain_b[...], gain_b[...]], axis=1)
        encoded = (hidden * scale * gains).astype(BF16)
        e_tmp[...] = encoded
        own = e_tmp[pl.ds(pl.multiple_of(sp * HEAD, HEAD), HEAD), :]
        e_t[b0] = own[:, :TOK]
        e_t[b1] = own[:, TOK:]
        key = mm(kp_t[...], encoded).astype(BF16)
        k_t[b0] = key[:, :TOK]
        k_t[b1] = key[:, TOK:]
        mark = jnp.concatenate([hot[b0], hot[b1]], axis=1)
        mark = jnp.concatenate([mark, mark, mark], axis=0)
        told = (encoded.astype(F32) + mm(tab_t[...], mark)).astype(BF16)
        value = mm(vp_t[...], told).astype(BF16)
        state[...] += mm_nt(value, key).reshape(OWNERS, 8, FEAT)

    state[...] = state[...] * (BANDS * TOK) ** -0.5

    to_owners(lambda c: state.at[c], states, 4, state_in)

    @pl.when(is_owner)
    def _():
        states[tm] = state[tm // STRIDE]
        decays[tm] = decay_own[...]
        arrived(decays.at[pl.ds(0, FRAMES - 1)], decay_in)
        arrived(states.at[pl.ds(0, FRAMES - 1)], state_in)
        place = tm // STRIDE

        def frame(t, held):
            held = decays[t] * held
            memories[t] = held

            @pl.when(t != tm)
            def _():
                pltpu.make_async_remote_copy(
                    src_ref=memories.at[t],
                    dst_ref=memory.at[place],
                    send_sem=send.at[5],
                    recv_sem=memory_in,
                    device_id=(t, sp),
                    device_id_type=MESH,
                ).start()

            return held + states[t]

        lax.fori_loop(0, FRAMES, frame, jnp.zeros((8, FEAT), F32))
        memory[place] = memories[tm]
        arrived(memory.at[pl.ds(0, OWNERS - 1)], memory_in)

    @pl.when(jnp.logical_not(is_owner))
    def _():
        arrived(memory, memory_in)

    now = memory[...].reshape(FEAT, FEAT).astype(BF16)
    for p in range(BANDS // 2):
        key = jnp.concatenate([k_t[2 * p], k_t[2 * p + 1]], axis=1)
        own = jnp.concatenate([e_t[2 * p], e_t[2 * p + 1]], axis=1)
        read = (mm(now, key) * FEAT**-0.5).astype(BF16)
        c = mm(taps_t[...], jnp.concatenate([read, own], axis=0))
        conved[2 * p] = c[:, :TOK]
        conved[2 * p + 1] = c[:, TOK:]
    lane = iota((CH, TOK), 1)
    column = lax.rem(lane, 64)

    def tap(n, a, b):
        at = (a * 3 + b) * CH
        return conved[n, at : at + CH, :]

    for n in range(BANDS):
        shifted = []
        for b in range(3):
            late, early = tap(n, 2, b), tap(n, 0, b)
            if n > 0:
                late = late + tap(n - 1, 0, b)
            if n < BANDS - 1:
                early = early + tap(n + 1, 2, b)
            shifted.append(tap(n, 1, b) + pltpu.roll(jnp.where(lane >= 64, late, early), 64, 1))
        total = shifted[1]
        total = total + jnp.where(column != 63, pltpu.roll(shifted[2], TOK - 1, 1), 0.0)
        total = total + jnp.where(column != 0, pltpu.roll(shifted[0], 1, 1), 0.0)
        part[n] = total.astype(BF16)

        @pl.when(sp != n)
        def _():
            pltpu.make_async_remote_copy(
                src_ref=part.at[n],
                dst_ref=parts.at[sp],
                send_sem=send.at[6],
                recv_sem=part_in,
                device_id=(tm, n),
                device_id_type=MESH,
            ).start()

    parts[sp] = part[sp]
    arrived(parts.at[pl.ds(0, BANDS - 1)], part_in)
    total = parts[0].astype(F32)
    for n in range(1, BANDS):
        total = total + parts[n].astype(F32)
    cubic = total + 0.044715 * (total * total * total)
    hidden = (0.5 * total * (1.0 + jnp.tanh(math.sqrt(2 / math.pi) * cubic))).astype(BF16)
    pixels = mm(up_x[...], hidden)
    keep = (lax.rem(iota((32, TOK), 0) // 4, 2)) == (iota((32, TOK), 1) // 64)
    pixels = jnp.where(keep, pixels, 0.0)
    wide = jnp.concatenate([pixels[8 * b : 8 * b + 8] for b in range(4)], axis=1)
    high, middle, low = three_parts(wide)
    high = mm(high, spread[...])
    out[0] = high + (mm(middle, spread[...]) + mm(low, spread[...]))

    arrived(pool.at[pl.ds(0, BANDS - 1)], send.at[0])
    arrived(hot.at[pl.ds(0, BANDS - 1)], send.at[1])
    arrived(xt.at[pl.ds(0, BANDS - 1)], send.at[2])

    @pl.when(is_owner)
    def _():
        arrived(state.at[pl.ds(0, OWNERS - 1)], send.at[3])
        arrived(state.at[pl.ds(0, OWNERS - 1)], send.at[4])
        arrived(memories.at[pl.ds(0, FRAMES - 1)], send.at[5])

    @pl.when(jnp.logical_not(is_owner))
    def _():
        arrived(state, send.at[3])
        arrived(state, send.at[4])

    arrived(part.at[pl.ds(0, BANDS - 1)], send.at[6])


def shards(frames, labels, table, qkv, eo, gain, kp, vp, rp, decay, conv, up):
    vmem = pltpu.VMEM
    dma = pltpu.SemaphoreType.DMA
    scratch = [
        vmem((2, 64, DIM), BF16), vmem((2, 64), jnp.int32), vmem((4, DIM), F32),
        vmem((DIM, 3 * DIM), BF16), vmem((DIM, DIM), BF16), vmem((1, DIM), F32),
        vmem((DIM, FEAT), BF16), vmem((DIM, FEAT), BF16), vmem((FEAT, DIM), BF16),
        vmem((1, HEADS), F32), vmem((TAPS, CH, DIM), BF16), vmem((16, CH), BF16),
        vmem((DIM, DIM), BF16), vmem((DIM, DIM), BF16), vmem((FEAT, DIM), BF16),
        vmem((FEAT, DIM), BF16), vmem((DIM, 48), BF16), vmem((DIM, TOK), F32),
        vmem((TAPS * CH, FEAT + HEAD), BF16), vmem((32, CH), BF16), vmem((4 * TOK, DIM), BF16),
        vmem((BANDS, TOK // 4, DIM), BF16), vmem((BANDS, 16, TOK), BF16),
        vmem((BANDS, DIM, TOK), BF16), vmem((HEADS * DIM, DIM), BF16),
        vmem((DIM, HEADS * DIM), BF16), vmem((HEADS * DIM, 2 * TOK), BF16),
        vmem((BANDS, HEAD, TOK), BF16), vmem((DIM, 2 * TOK), BF16), vmem((BANDS, FEAT, TOK), BF16),
        vmem((OWNERS, 8, FEAT), F32), vmem((FRAMES, 8, FEAT), F32), vmem((FRAMES, 8, FEAT), F32),
        vmem((8, FEAT), F32), vmem((FRAMES, 8, FEAT), F32), vmem((OWNERS, 8, FEAT), F32),
        vmem((BANDS, TAPS * CH, TOK), F32), vmem((BANDS, CH, TOK), BF16),
        vmem((BANDS, CH, TOK), BF16),
        dma((12,)), dma((7,)), dma, dma, dma((BANDS,)), dma, dma, dma, dma,
    ]
    return pl.pallas_call(
        kernel,
        out_shape=jax.ShapeDtypeStruct((1, 8, DIM), F32),
        in_specs=[pl.BlockSpec(memory_space=pltpu.HBM)] * 12,
        out_specs=pl.BlockSpec(memory_space=pltpu.VMEM),
        scratch_shapes=scratch,
        compiler_params=pltpu.CompilerParams(
            collective_id=0, has_side_effects=True, vmem_limit_bytes=63 * 1024 * 1024
        ),
        name="propagate",
    )(
        frames, labels, table, qkv, eo, gain.reshape(1, DIM), kp, vp, rp, decay,
        conv.transpose(0, 1, 3, 2).reshape(TAPS, CH, DIM), up.T,
    )


def solution(mesh):
    return jax.shard_map(
        shards,
        mesh=mesh,
        in_specs=(
            P("tm", "space", None, None), P("space", None), P(), P(), P(), P(), P(), P(), P(),
            P("tm", None), P(), P(),
        ),
        out_specs=P("tm", "space", None),
        check_vma=False,
    )
```

```python
import math

import jax
import jax.numpy as jnp
from jax import lax
from jax.experimental import pallas as pl
from jax.experimental.pallas import tpu as pltpu
from jax.sharding import PartitionSpec as P

MESH = pl.DeviceIdType.MESH
BF16 = jnp.bfloat16
F32 = jnp.float32

FRAMES = 64
BANDS = 8
OWNERS = 16
STRIDE = FRAMES // OWNERS
TOK = 128
DIM = 256
HEADS = 8
HEAD = DIM // HEADS
FEAT = 128
CH = 64
TAPS = 9
SERVED = 3
FAR_FIRST = (4, 3, 5, 2, 6, 1, 7)


def mm(a, b):
    return jnp.dot(a, b, preferred_element_type=F32)


def mm_nt(a, b):
    return lax.dot_general(a, b, (((1,), (1,)), ((), ())), preferred_element_type=F32)


def turned(x):
    return x.astype(F32).T.astype(x.dtype)


def iota(shape, dim):
    return lax.broadcasted_iota(jnp.int32, shape, dim)


def three_parts(x):
    high = x.astype(BF16)
    rest = x - high.astype(F32)
    middle = rest.astype(BF16)
    low = (rest - middle.astype(F32)).astype(BF16)
    return high, middle, low


def kernel(
    frames, labels, table, qkv, eo, gain, kp, vp, rp, decay, conv, up,
    out,
    x_v, lab_v, tab_v, qkv_v, eo_v, gain_v, kp_v, vp_v, rp_v, dec_v, conv_v, up_v,
    wq_t, eo_t, kp_t, vp_t, tab_t, gain_b, taps_t, up_x, spread,
    pool, hot, xt, kmask, v_mask, weights, e_tmp, state_out, state_part, ke_out, ke,
    state, states, decays, decay_own, memories, memory,
    conved, part, parts,
    load, send, pool_in, hot_in, xt_in, part_state_in, ke_in, decay_in, state_in, memory_in, part_in,
):
    tm, sp = lax.axis_index("tm"), lax.axis_index("space")
    is_owner = lax.rem(tm, STRIDE) == 0
    side, pair = lax.rem(sp, 2), sp // 2
    heads = [sp] + [lax.rem(sp + BANDS + (2 * side - 1) * k, BANDS) for k in range(1, SERVED + 1)]

    barrier = pltpu.get_barrier_semaphore()
    for k in range(1, BANDS):
        pl.semaphore_signal(
            barrier, inc=1, device_id=(tm, lax.rem(sp + k, BANDS)), device_id_type=MESH
        )

    @pl.when(is_owner)
    def _():
        @pl.loop(1, FRAMES)
        def _(k):
            pl.semaphore_signal(
                barrier, inc=1, device_id=(lax.rem(tm + k, FRAMES), sp), device_id_type=MESH
            )

    @pl.when(jnp.logical_not(is_owner))
    def _():
        @pl.loop(0, OWNERS)
        def _(k):
            pl.semaphore_signal(barrier, inc=1, device_id=(k * STRIDE, sp), device_id_type=MESH)

    col = pl.multiple_of(sp * FEAT, FEAT)
    loads = [
        (frames.at[0], x_v),
        (labels, lab_v),
        (decay, dec_v),
        (qkv, qkv_v),
        (table, tab_v),
        (eo, eo_v),
        (gain, gain_v),
        (rp.at[pl.ds(col, FEAT), :], rp_v),
        (conv, conv_v),
        (up, up_v),
    ]
    for k, h in enumerate(heads):
        at = pl.ds(pl.multiple_of(h * FEAT, FEAT), FEAT)
        loads.append((kp.at[:, at], kp_v.at[k]))
        loads.append((vp.at[:, at], vp_v.at[k]))
    loads = [pltpu.make_async_copy(s, d, load.at[n]) for n, (s, d) in enumerate(loads)]
    for c in loads:
        c.start()

    loads[0].wait()
    x = x_v[...].reshape(TOK, DIM)
    pr, pc = iota((TOK // 4, TOK), 0), iota((TOK // 4, TOK), 1)
    quarter = jnp.where(lax.rem(pc, 64) // 2 == pr, 0.25, 0.0).astype(BF16)
    pool[sp] = mm(quarter, x).astype(BF16)
    loads[1].wait()
    lab = lab_v[...]
    lab_row = jnp.concatenate([lab[0:1], lab[1:2]], axis=1)
    hit = (jnp.broadcast_to(lab_row, (16, TOK)) == iota((16, TOK), 0)) & (tm == 0)
    hot[side] = jnp.where(hit, 1.0, 0.0).astype(BF16)
    loads[2].wait()
    rate = jnp.sum(
        jnp.where(iota((1, HEADS), 1) == sp, dec_v[...], 0.0), axis=1, keepdims=True
    )
    decay_own[...] = jnp.broadcast_to(rate, (8, FEAT))

    @pl.when(is_owner)
    def _():
        pl.semaphore_wait(barrier, BANDS - 1 + FRAMES - 1)

    @pl.when(jnp.logical_not(is_owner))
    def _():
        pl.semaphore_wait(barrier, BANDS - 1 + OWNERS)

    def to_band(place, src, dst, n, sem):
        pltpu.make_async_remote_copy(
            src_ref=src,
            dst_ref=dst,
            send_sem=send.at[n],
            recv_sem=sem,
            device_id=(tm, place),
            device_id_type=MESH,
        ).start()

    def arrived(ref, sem):
        pltpu.make_async_copy(ref, ref, sem).wait()

    for k in FAR_FIRST:
        to_band(lax.rem(sp + k, BANDS), pool.at[sp], pool.at[sp], 0, pool_in)
    xt[side] = x.astype(F32).T.astype(BF16)
    to_band(sp + 1 - 2 * side, xt.at[side], xt.at[side], 2, xt_in)
    to_band(sp + 1 - 2 * side, hot.at[side], hot.at[side], 1, hot_in)

    def to_owners(src, dst, n, sem):
        for c in range(OWNERS):
            @pl.when(tm != c * STRIDE)
            def _():
                pltpu.make_async_remote_copy(
                    src_ref=src(c),
                    dst_ref=dst.at[tm],
                    send_sem=send.at[n],
                    recv_sem=sem,
                    device_id=(c * STRIDE, sp),
                    device_id_type=MESH,
                ).start()

    to_owners(lambda c: decay_own, decays, 3, decay_in)

    for c in loads[3:]:
        c.wait()
    wq_t[...] = turned(qkv_v[:, :DIM])
    eo_t[...] = turned(eo_v[...])
    for k in range(SERVED + 1):
        kp_t[k * FEAT : (k + 1) * FEAT, :] = turned(kp_v[k])
        vp_t[k * FEAT : (k + 1) * FEAT, :] = turned(vp_v[k])
    tab = jnp.concatenate([tab_v[...], jnp.zeros((12, DIM), F32)], axis=0)
    tab_t[...] = turned(jnp.concatenate(three_parts(tab), axis=0))
    gain_b[...] = jnp.broadcast_to(gain_v[...], (TOK, DIM)).T

    here = jnp.where(iota((DIM, HEAD), 0) == sp * HEAD + iota((DIM, HEAD), 1), 1.0, 0.0).astype(BF16)

    @pl.loop(0, TAPS)
    def _(n):
        both = mm_nt(conv_v[n], rp_v[...]).astype(BF16)
        own = mm(conv_v[n], here).astype(BF16)
        taps_t[pl.ds(pl.multiple_of(n * CH, CH), CH), :] = jnp.concatenate([both, own], axis=1)

    row, src_row = iota((32, 16), 0), iota((32, 16), 1)
    picks = jnp.where(src_row == 4 * lax.rem(row, 4) + row // 8, 1.0, 0.0).astype(BF16)
    up_x[...] = mm(picks, up_v[...]).astype(BF16)
    er, ec = iota((4 * TOK, DIM), 0), iota((4 * TOK, DIM), 1)
    spread[...] = jnp.where(ec == 4 * lax.rem(er, 64) + er // TOK, 1.0, 0.0).astype(BF16)

    arrived(pool.at[pl.ds(0, BANDS - 1)], pool_in)
    pooled = pool[...].reshape(BANDS * TOK // 4, DIM)
    kv = mm(pooled, qkv_v[:, DIM:])
    keys = kv[:, :DIM].astype(BF16)
    values = kv[:, DIM:].T.astype(BF16)
    lane_head, row_head = iota((DIM, DIM), 1) // HEAD, iota((DIM, DIM), 0) // HEAD
    for h in range(HEADS):
        kmask[h * DIM : (h + 1) * DIM, :] = jnp.where(lane_head == h, keys, jnp.zeros_like(keys))
        v_mask[:, h * DIM : (h + 1) * DIM] = jnp.where(row_head == h, values, jnp.zeros_like(values))

    factor = HEAD**-0.5 * math.log2(math.e)
    arrived(xt.at[0], xt_in)
    arrived(hot.at[0], hot_in)
    xp = jnp.concatenate([xt[0], xt[1]], axis=1)
    q = mm(wq_t[...], xp).astype(BF16)
    scores = mm(kmask[...], q)
    inverse = []
    for h in range(HEADS):
        s = scores[h * DIM : (h + 1) * DIM]
        w = jnp.exp2((s - jnp.max(s, axis=0, keepdims=True)) * factor)
        inverse.append(
            jnp.broadcast_to(1.0 / jnp.sum(w, axis=0, keepdims=True), (HEAD, 2 * TOK))
        )
        weights[h * DIM : (h + 1) * DIM, :] = w.astype(BF16)
    summed = mm(v_mask[...], weights[...])
    attended = (summed * jnp.concatenate(inverse, axis=0)).astype(BF16)
    hidden = xp.astype(F32) + mm(eo_t[...], attended)
    scale = lax.rsqrt(jnp.mean(hidden * hidden, axis=0, keepdims=True) + 1e-06)
    gains = jnp.concatenate([gain_b[...], gain_b[...]], axis=1)
    encoded = (hidden * scale * gains).astype(BF16)
    e_tmp[...] = encoded
    mark = jnp.concatenate([hot[0], hot[1]], axis=1)
    mark = jnp.concatenate([mark, mark, mark], axis=0)
    told = (encoded.astype(F32) + mm(tab_t[...], mark)).astype(BF16)
    keys = mm(kp_t[...], encoded).astype(BF16)
    values = mm(vp_t[...], told).astype(BF16)

    def share(k):
        at = slice(k * FEAT, (k + 1) * FEAT)
        return mm_nt(values[at], keys[at]) * (BANDS * TOK) ** -0.5

    for k in range(SERVED, 0, -1):
        state_out[k - 1] = share(k).astype(BF16)
        to_band(heads[k], state_out.at[k - 1], state_part.at[k - 1], 7, part_state_in)
    total = share(0)
    for k in range(SERVED + 1):
        h = pl.multiple_of(heads[k] * HEAD, HEAD)
        both = jnp.concatenate([keys[k * FEAT : (k + 1) * FEAT], e_tmp[pl.ds(h, HEAD), :]], axis=0)
        if k == 0:
            ke[pair] = both
        else:
            ke_out[k - 1] = both
            to_band(heads[k], ke_out.at[k - 1], ke.at[pair], 8, ke_in)
    arrived(state_part, part_state_in)
    for k in range(SERVED):
        total = total + state_part[k].astype(F32)
    state[...] = total.reshape(OWNERS, 8, FEAT)

    to_owners(lambda c: state.at[c], states, 4, state_in)

    @pl.when(is_owner)
    def _():
        states[tm] = state[tm // STRIDE]
        decays[tm] = decay_own[...]
        arrived(decays.at[pl.ds(0, FRAMES - 1)], decay_in)
        arrived(states.at[pl.ds(0, FRAMES - 1)], state_in)
        place = tm // STRIDE

        def frame(t, held):
            held = decays[t] * held
            memories[t] = held

            @pl.when(t != tm)
            def _():
                pltpu.make_async_remote_copy(
                    src_ref=memories.at[t],
                    dst_ref=memory.at[place],
                    send_sem=send.at[5],
                    recv_sem=memory_in,
                    device_id=(t, sp),
                    device_id_type=MESH,
                ).start()

            return held + states[t]

        lax.fori_loop(0, FRAMES, frame, jnp.zeros((8, FEAT), F32))
        memory[place] = memories[tm]
        arrived(memory.at[pl.ds(0, OWNERS - 1)], memory_in)

    @pl.when(jnp.logical_not(is_owner))
    def _():
        arrived(memory, memory_in)

    now = memory[...].reshape(FEAT, FEAT).astype(BF16)
    arrived(ke_out, ke_in)
    for p in range(BANDS // 2):
        read = (mm(now, ke[p, :FEAT, :]) * FEAT**-0.5).astype(BF16)
        c = mm(taps_t[...], jnp.concatenate([read, ke[p, FEAT:, :]], axis=0))
        conved[2 * p] = c[:, :TOK]
        conved[2 * p + 1] = c[:, TOK:]
    lane = iota((CH, TOK), 1)
    column = lax.rem(lane, 64)

    def tap(n, a, b):
        at = (a * 3 + b) * CH
        return conved[n, at : at + CH, :]

    for n in range(BANDS):
        shifted = []
        for b in range(3):
            late, early = tap(n, 2, b), tap(n, 0, b)
            if n > 0:
                late = late + tap(n - 1, 0, b)
            if n < BANDS - 1:
                early = early + tap(n + 1, 2, b)
            shifted.append(tap(n, 1, b) + pltpu.roll(jnp.where(lane >= 64, late, early), 64, 1))
        total = shifted[1]
        total = total + jnp.where(column != 63, pltpu.roll(shifted[2], TOK - 1, 1), 0.0)
        total = total + jnp.where(column != 0, pltpu.roll(shifted[0], 1, 1), 0.0)
        part[n] = total.astype(BF16)

        @pl.when(sp != n)
        def _():
            pltpu.make_async_remote_copy(
                src_ref=part.at[n],
                dst_ref=parts.at[sp],
                send_sem=send.at[6],
                recv_sem=part_in,
                device_id=(tm, n),
                device_id_type=MESH,
            ).start()

    parts[sp] = part[sp]
    arrived(parts.at[pl.ds(0, BANDS - 1)], part_in)
    total = parts[0].astype(F32)
    for n in range(1, BANDS):
        total = total + parts[n].astype(F32)
    cubic = total + 0.044715 * (total * total * total)
    hidden = (0.5 * total * (1.0 + jnp.tanh(math.sqrt(2 / math.pi) * cubic))).astype(BF16)
    pixels = mm(up_x[...], hidden)
    keep = (lax.rem(iota((32, TOK), 0) // 4, 2)) == (iota((32, TOK), 1) // 64)
    pixels = jnp.where(keep, pixels, 0.0)
    wide = jnp.concatenate([pixels[8 * b : 8 * b + 8] for b in range(4)], axis=1)
    high, middle, low = three_parts(wide)
    high = mm(high, spread[...])
    out[0] = high + (mm(middle, spread[...]) + mm(low, spread[...]))

    arrived(pool.at[pl.ds(0, BANDS - 1)], send.at[0])
    arrived(hot.at[0], send.at[1])
    arrived(xt.at[0], send.at[2])
    arrived(state_out, send.at[7])
    arrived(ke_out, send.at[8])

    @pl.when(is_owner)
    def _():
        arrived(state.at[pl.ds(0, OWNERS - 1)], send.at[3])
        arrived(state.at[pl.ds(0, OWNERS - 1)], send.at[4])
        arrived(memories.at[pl.ds(0, FRAMES - 1)], send.at[5])

    @pl.when(jnp.logical_not(is_owner))
    def _():
        arrived(state, send.at[3])
        arrived(state, send.at[4])

    arrived(part.at[pl.ds(0, BANDS - 1)], send.at[6])


def shards(frames, labels, table, qkv, eo, gain, kp, vp, rp, decay, conv, up):
    vmem = pltpu.VMEM
    dma = pltpu.SemaphoreType.DMA
    scratch = [
        vmem((2, 64, DIM), BF16), vmem((2, 64), jnp.int32), vmem((4, DIM), F32),
        vmem((DIM, 3 * DIM), BF16), vmem((DIM, DIM), BF16), vmem((1, DIM), F32),
        vmem((SERVED + 1, DIM, FEAT), BF16), vmem((SERVED + 1, DIM, FEAT), BF16), vmem((FEAT, DIM), BF16),
        vmem((1, HEADS), F32), vmem((TAPS, CH, DIM), BF16), vmem((16, CH), BF16),
        vmem((DIM, DIM), BF16), vmem((DIM, DIM), BF16), vmem(((SERVED + 1) * FEAT, DIM), BF16),
        vmem(((SERVED + 1) * FEAT, DIM), BF16), vmem((DIM, 48), BF16), vmem((DIM, TOK), F32),
        vmem((TAPS * CH, FEAT + HEAD), BF16), vmem((32, CH), BF16), vmem((4 * TOK, DIM), BF16),
        vmem((BANDS, TOK // 4, DIM), BF16), vmem((2, 16, TOK), BF16),
        vmem((2, DIM, TOK), BF16), vmem((HEADS * DIM, DIM), BF16),
        vmem((DIM, HEADS * DIM), BF16), vmem((HEADS * DIM, 2 * TOK), BF16),
        vmem((DIM, 2 * TOK), BF16), vmem((SERVED, FEAT, FEAT), BF16), vmem((SERVED, FEAT, FEAT), BF16),
        vmem((SERVED, FEAT + HEAD, 2 * TOK), BF16), vmem((BANDS // 2, FEAT + HEAD, 2 * TOK), BF16),
        vmem((OWNERS, 8, FEAT), F32), vmem((FRAMES, 8, FEAT), F32), vmem((FRAMES, 8, FEAT), F32),
        vmem((8, FEAT), F32), vmem((FRAMES, 8, FEAT), F32), vmem((OWNERS, 8, FEAT), F32),
        vmem((BANDS, TAPS * CH, TOK), F32), vmem((BANDS, CH, TOK), BF16),
        vmem((BANDS, CH, TOK), BF16),
        dma((18,)), dma((9,)), dma, dma, dma, dma, dma, dma, dma, dma, dma,
    ]
    return pl.pallas_call(
        kernel,
        out_shape=jax.ShapeDtypeStruct((1, 8, DIM), F32),
        in_specs=[pl.BlockSpec(memory_space=pltpu.HBM)] * 12,
        out_specs=pl.BlockSpec(memory_space=pltpu.VMEM),
        scratch_shapes=scratch,
        compiler_params=pltpu.CompilerParams(
            collective_id=0, has_side_effects=True, vmem_limit_bytes=63 * 1024 * 1024
        ),
        name="propagate",
    )(
        frames, labels, table, qkv, eo, gain.reshape(1, DIM), kp, vp, rp, decay,
        conv.transpose(0, 1, 3, 2).reshape(TAPS, CH, DIM), up.T,
    )


def solution(mesh):
    return jax.shard_map(
        shards,
        mesh=mesh,
        in_specs=(
            P("tm", "space", None, None), P("space", None), P(), P(), P(), P(), P(), P(), P(),
            P("tm", None), P(), P(),
        ),
        out_specs=P("tm", "space", None),
        check_vma=False,
    )
```

```python
import math

import jax
import jax.numpy as jnp
from jax import lax
from jax.experimental import pallas as pl
from jax.experimental.pallas import tpu as pltpu
from jax.sharding import PartitionSpec as P

MESH = pl.DeviceIdType.MESH
BF16 = jnp.bfloat16
F32 = jnp.float32

FRAMES = 64
BANDS = 8
OWNERS = 16
STRIDE = FRAMES // OWNERS
TOK = 128
DIM = 256
HEADS = 8
HEAD = DIM // HEADS
FEAT = 128
CH = 64
TAPS = 9
SERVED = 3
FAR_FIRST = (4, 3, 5, 2, 6, 1, 7)


def mm(a, b):
    return jnp.dot(a, b, preferred_element_type=F32)


def mm_nt(a, b):
    return lax.dot_general(a, b, (((1,), (1,)), ((), ())), preferred_element_type=F32)


def turned(x):
    return x.astype(F32).T.astype(x.dtype)


def iota(shape, dim):
    return lax.broadcasted_iota(jnp.int32, shape, dim)


def three_parts(x):
    high = x.astype(BF16)
    rest = x - high.astype(F32)
    middle = rest.astype(BF16)
    low = (rest - middle.astype(F32)).astype(BF16)
    return high, middle, low


def kernel(
    frames, labels, table, qkv, eo, gain, kp, vp, rp, decay, conv, up,
    out,
    x_v, lab_v, tab_v, qkv_v, eo_v, gain_v, kp_v, vp_v, rp_v, dec_v, conv_v, up_v,
    wq_t, eo_t, kp_t, vp_t, tab_t, gain_b, taps_t, up_x, spread,
    pool, hot, xt, kmask, v_mask, weights, e_tmp, state_out, state_part, ke_out, ke,
    state, states, decays, decay_own, memories, memory,
    conved, part, parts,
    load, send, greetings, pool_in, hot_in, xt_in, part_state_in, ke_in, decay_in, state_in, memory_in, part_in,
):
    tm, sp = lax.axis_index("tm"), lax.axis_index("space")
    is_owner = lax.rem(tm, STRIDE) == 0
    side, pair = lax.rem(sp, 2), sp // 2
    heads = [sp] + [lax.rem(sp + BANDS + (2 * side - 1) * k, BANDS) for k in range(1, SERVED + 1)]

    core, y, x = lax.rem(tm, 2), lax.rem(tm // 2, 8), tm // 16
    along_y = [x * 16 + lax.rem(y + k, 8) * 2 + core for k in (1, 7)]
    along_x = [lax.rem(x + k, 4) * 16 + y * 2 + core for k in (1, 3)]

    barrier = pltpu.get_barrier_semaphore()
    for k in range(1, BANDS):
        pl.semaphore_signal(
            barrier, inc=1, device_id=(tm, lax.rem(sp + k, BANDS)), device_id_type=MESH
        )

    partner = 1 - 2 * core
    for t in (*along_y, *along_x, *(t + partner for t in along_y), tm + partner):
        pl.semaphore_signal(barrier, inc=1, device_id=(t, sp), device_id_type=MESH)

    def greet(n):
        for t in along_y if n < 3 else along_x:
            pl.semaphore_signal(
                greetings.at[n], inc=1, device_id=(t, sp), device_id_type=MESH
            )

    def greeted(n):
        pl.semaphore_wait(greetings.at[n], 2)

    col = pl.multiple_of(sp * FEAT, FEAT)
    loads = [
        (frames.at[0], x_v),
        (labels, lab_v),
        (decay, dec_v),
        (qkv, qkv_v),
        (table, tab_v),
        (eo, eo_v),
        (gain, gain_v),
        (rp.at[pl.ds(col, FEAT), :], rp_v),
        (conv, conv_v),
        (up, up_v),
    ]
    for k, h in enumerate(heads):
        at = pl.ds(pl.multiple_of(h * FEAT, FEAT), FEAT)
        loads.append((kp.at[:, at], kp_v.at[k]))
        loads.append((vp.at[:, at], vp_v.at[k]))
    loads = [pltpu.make_async_copy(s, d, load.at[n]) for n, (s, d) in enumerate(loads)]
    for c in loads:
        c.start()

    loads[0].wait()
    own = x_v[...].reshape(TOK, DIM)
    pr, pc = iota((TOK // 4, TOK), 0), iota((TOK // 4, TOK), 1)
    quarter = jnp.where(lax.rem(pc, 64) // 2 == pr, 0.25, 0.0).astype(BF16)
    pool[sp] = mm(quarter, own).astype(BF16)
    loads[1].wait()
    lab = lab_v[...]
    lab_row = jnp.concatenate([lab[0:1], lab[1:2]], axis=1)
    hit = (jnp.broadcast_to(lab_row, (16, TOK)) == iota((16, TOK), 0)) & (tm == 0)
    hot[side] = jnp.where(hit, 1.0, 0.0).astype(BF16)
    loads[2].wait()
    rate = jnp.sum(
        jnp.where(iota((1, HEADS), 1) == sp, dec_v[...], 0.0), axis=1, keepdims=True
    )
    decay_own[...] = jnp.broadcast_to(rate, (8, FEAT))

    pl.semaphore_wait(barrier, BANDS - 1 + 7)

    def to_band(place, src, dst, n, sem):
        pltpu.make_async_remote_copy(
            src_ref=src,
            dst_ref=dst,
            send_sem=send.at[n],
            recv_sem=sem,
            device_id=(tm, place),
            device_id_type=MESH,
        ).start()

    def arrived(ref, sem):
        pltpu.make_async_copy(ref, ref, sem).wait()

    for k in FAR_FIRST:
        to_band(lax.rem(sp + k, BANDS), pool.at[sp], pool.at[sp], 0, pool_in)
    xt[side] = own.astype(F32).T.astype(BF16)
    to_band(sp + 1 - 2 * side, xt.at[side], xt.at[side], 2, xt_in)
    to_band(sp + 1 - 2 * side, hot.at[side], hot.at[side], 1, hot_in)

    def to_owners(src, dst, n, sem):
        for c in range(OWNERS):
            @pl.when(tm != c * STRIDE)
            def _():
                pltpu.make_async_remote_copy(
                    src_ref=src(c),
                    dst_ref=dst.at[tm],
                    send_sem=send.at[n],
                    recv_sem=sem,
                    device_id=(c * STRIDE, sp),
                    device_id_type=MESH,
                ).start()

    greet(0)
    for c in loads[3:]:
        c.wait()
    wq_t[...] = turned(qkv_v[:, :DIM])
    eo_t[...] = turned(eo_v[...])
    greeted(0)
    greet(1)
    for k in range(SERVED + 1):
        kp_t[k * FEAT : (k + 1) * FEAT, :] = turned(kp_v[k])
        vp_t[k * FEAT : (k + 1) * FEAT, :] = turned(vp_v[k])
    greeted(1)
    greet(2)
    tab = jnp.concatenate([tab_v[...], jnp.zeros((12, DIM), F32)], axis=0)
    tab_t[...] = turned(jnp.concatenate(three_parts(tab), axis=0))
    gain_b[...] = jnp.broadcast_to(gain_v[...], (TOK, DIM)).T

    arrived(pool.at[pl.ds(0, BANDS - 1)], pool_in)
    pooled = pool[...].reshape(BANDS * TOK // 4, DIM)
    kv = mm(pooled, qkv_v[:, DIM:])
    keys = kv[:, :DIM].astype(BF16)
    values = kv[:, DIM:].T.astype(BF16)
    lane_head, row_head = iota((DIM, DIM), 1) // HEAD, iota((DIM, DIM), 0) // HEAD
    for h in range(HEADS):
        kmask[h * DIM : (h + 1) * DIM, :] = jnp.where(lane_head == h, keys, jnp.zeros_like(keys))
        v_mask[:, h * DIM : (h + 1) * DIM] = jnp.where(row_head == h, values, jnp.zeros_like(values))

    greeted(2)
    greet(3)

    factor = HEAD**-0.5 * math.log2(math.e)
    arrived(xt.at[0], xt_in)
    arrived(hot.at[0], hot_in)
    xp = jnp.concatenate([xt[0], xt[1]], axis=1)
    q = mm(wq_t[...], xp).astype(BF16)
    scores = mm(kmask[...], q)
    inverse = []
    for h in range(HEADS):
        s = scores[h * DIM : (h + 1) * DIM]
        w = jnp.exp2((s - jnp.max(s, axis=0, keepdims=True)) * factor)
        inverse.append(
            jnp.broadcast_to(1.0 / jnp.sum(w, axis=0, keepdims=True), (HEAD, 2 * TOK))
        )
        weights[h * DIM : (h + 1) * DIM, :] = w.astype(BF16)
    summed = mm(v_mask[...], weights[...])
    attended = (summed * jnp.concatenate(inverse, axis=0)).astype(BF16)
    greeted(3)
    greet(4)
    hidden = xp.astype(F32) + mm(eo_t[...], attended)
    scale = lax.rsqrt(jnp.mean(hidden * hidden, axis=0, keepdims=True) + 1e-06)
    gains = jnp.concatenate([gain_b[...], gain_b[...]], axis=1)
    encoded = (hidden * scale * gains).astype(BF16)
    e_tmp[...] = encoded
    mark = jnp.concatenate([hot[0], hot[1]], axis=1)
    mark = jnp.concatenate([mark, mark, mark], axis=0)
    told = (encoded.astype(F32) + mm(tab_t[...], mark)).astype(BF16)
    keys = mm(kp_t[...], encoded).astype(BF16)
    values = mm(vp_t[...], told).astype(BF16)

    def share(k):
        at = slice(k * FEAT, (k + 1) * FEAT)
        return mm_nt(values[at], keys[at]) * (BANDS * TOK) ** -0.5

    for k in range(SERVED, 0, -1):
        state_out[k - 1] = share(k).astype(BF16)
        to_band(heads[k], state_out.at[k - 1], state_part.at[k - 1], 7, part_state_in)
    total = share(0)
    for k in range(SERVED + 1):
        h = pl.multiple_of(heads[k] * HEAD, HEAD)
        both = jnp.concatenate([keys[k * FEAT : (k + 1) * FEAT], e_tmp[pl.ds(h, HEAD), :]], axis=0)
        if k == 0:
            ke[pair] = both
        else:
            ke_out[k - 1] = both
            to_band(heads[k], ke_out.at[k - 1], ke.at[pair], 8, ke_in)
    greeted(4)
    to_owners(lambda c: decay_own, decays, 3, decay_in)

    here = jnp.where(iota((DIM, HEAD), 0) == sp * HEAD + iota((DIM, HEAD), 1), 1.0, 0.0).astype(BF16)

    @pl.loop(0, TAPS)
    def _(n):
        both = mm_nt(conv_v[n], rp_v[...]).astype(BF16)
        own = mm(conv_v[n], here).astype(BF16)
        taps_t[pl.ds(pl.multiple_of(n * CH, CH), CH), :] = jnp.concatenate([both, own], axis=1)

    row, src_row = iota((32, 16), 0), iota((32, 16), 1)
    picks = jnp.where(src_row == 4 * lax.rem(row, 4) + row // 8, 1.0, 0.0).astype(BF16)
    up_x[...] = mm(picks, up_v[...]).astype(BF16)
    er, ec = iota((4 * TOK, DIM), 0), iota((4 * TOK, DIM), 1)
    spread[...] = jnp.where(ec == 4 * lax.rem(er, 64) + er // TOK, 1.0, 0.0).astype(BF16)

    arrived(state_part, part_state_in)
    for k in range(SERVED):
        total = total + state_part[k].astype(F32)
    state[...] = total.reshape(OWNERS, 8, FEAT)

    to_owners(lambda c: state.at[c], states, 4, state_in)

    @pl.when(is_owner)
    def _():
        states[tm] = state[tm // STRIDE]
        decays[tm] = decay_own[...]
        arrived(decays.at[pl.ds(0, FRAMES - 1)], decay_in)
        arrived(states.at[pl.ds(0, FRAMES - 1)], state_in)
        place = tm // STRIDE

        def frame(t, held):
            held = decays[t] * held
            memories[t] = held

            @pl.when(t != tm)
            def _():
                pltpu.make_async_remote_copy(
                    src_ref=memories.at[t],
                    dst_ref=memory.at[place],
                    send_sem=send.at[5],
                    recv_sem=memory_in,
                    device_id=(t, sp),
                    device_id_type=MESH,
                ).start()

            return held + states[t]

        lax.fori_loop(0, FRAMES, frame, jnp.zeros((8, FEAT), F32))
        memory[place] = memories[tm]
        arrived(memory.at[pl.ds(0, OWNERS - 1)], memory_in)

    @pl.when(jnp.logical_not(is_owner))
    def _():
        arrived(memory, memory_in)

    now = memory[...].reshape(FEAT, FEAT).astype(BF16)
    arrived(ke_out, ke_in)
    for p in range(BANDS // 2):
        read = (mm(now, ke[p, :FEAT, :]) * FEAT**-0.5).astype(BF16)
        c = mm(taps_t[...], jnp.concatenate([read, ke[p, FEAT:, :]], axis=0))
        conved[2 * p] = c[:, :TOK]
        conved[2 * p + 1] = c[:, TOK:]
    lane = iota((CH, TOK), 1)
    column = lax.rem(lane, 64)

    def tap(n, a, b):
        at = (a * 3 + b) * CH
        return conved[n, at : at + CH, :]

    for n in range(BANDS):
        shifted = []
        for b in range(3):
            late, early = tap(n, 2, b), tap(n, 0, b)
            if n > 0:
                late = late + tap(n - 1, 0, b)
            if n < BANDS - 1:
                early = early + tap(n + 1, 2, b)
            shifted.append(tap(n, 1, b) + pltpu.roll(jnp.where(lane >= 64, late, early), 64, 1))
        total = shifted[1]
        total = total + jnp.where(column != 63, pltpu.roll(shifted[2], TOK - 1, 1), 0.0)
        total = total + jnp.where(column != 0, pltpu.roll(shifted[0], 1, 1), 0.0)
        part[n] = total.astype(BF16)

        @pl.when(sp != n)
        def _():
            pltpu.make_async_remote_copy(
                src_ref=part.at[n],
                dst_ref=parts.at[sp],
                send_sem=send.at[6],
                recv_sem=part_in,
                device_id=(tm, n),
                device_id_type=MESH,
            ).start()

    parts[sp] = part[sp]
    arrived(parts.at[pl.ds(0, BANDS - 1)], part_in)
    total = parts[0].astype(F32)
    for n in range(1, BANDS):
        total = total + parts[n].astype(F32)
    cubic = total + 0.044715 * (total * total * total)
    hidden = (0.5 * total * (1.0 + jnp.tanh(math.sqrt(2 / math.pi) * cubic))).astype(BF16)
    pixels = mm(up_x[...], hidden)
    keep = (lax.rem(iota((32, TOK), 0) // 4, 2)) == (iota((32, TOK), 1) // 64)
    pixels = jnp.where(keep, pixels, 0.0)
    wide = jnp.concatenate([pixels[8 * b : 8 * b + 8] for b in range(4)], axis=1)
    high, middle, low = three_parts(wide)
    high = mm(high, spread[...])
    out[0] = high + (mm(middle, spread[...]) + mm(low, spread[...]))

    arrived(pool.at[pl.ds(0, BANDS - 1)], send.at[0])
    arrived(hot.at[0], send.at[1])
    arrived(xt.at[0], send.at[2])
    arrived(state_out, send.at[7])
    arrived(ke_out, send.at[8])

    @pl.when(is_owner)
    def _():
        arrived(state.at[pl.ds(0, OWNERS - 1)], send.at[3])
        arrived(state.at[pl.ds(0, OWNERS - 1)], send.at[4])
        arrived(memories.at[pl.ds(0, FRAMES - 1)], send.at[5])

    @pl.when(jnp.logical_not(is_owner))
    def _():
        arrived(state, send.at[3])
        arrived(state, send.at[4])

    arrived(part.at[pl.ds(0, BANDS - 1)], send.at[6])


def shards(frames, labels, table, qkv, eo, gain, kp, vp, rp, decay, conv, up):
    vmem = pltpu.VMEM
    dma = pltpu.SemaphoreType.DMA
    scratch = [
        vmem((2, 64, DIM), BF16), vmem((2, 64), jnp.int32), vmem((4, DIM), F32),
        vmem((DIM, 3 * DIM), BF16), vmem((DIM, DIM), BF16), vmem((1, DIM), F32),
        vmem((SERVED + 1, DIM, FEAT), BF16), vmem((SERVED + 1, DIM, FEAT), BF16), vmem((FEAT, DIM), BF16),
        vmem((1, HEADS), F32), vmem((TAPS, CH, DIM), BF16), vmem((16, CH), BF16),
        vmem((DIM, DIM), BF16), vmem((DIM, DIM), BF16), vmem(((SERVED + 1) * FEAT, DIM), BF16),
        vmem(((SERVED + 1) * FEAT, DIM), BF16), vmem((DIM, 48), BF16), vmem((DIM, TOK), F32),
        vmem((TAPS * CH, FEAT + HEAD), BF16), vmem((32, CH), BF16), vmem((4 * TOK, DIM), BF16),
        vmem((BANDS, TOK // 4, DIM), BF16), vmem((2, 16, TOK), BF16),
        vmem((2, DIM, TOK), BF16), vmem((HEADS * DIM, DIM), BF16),
        vmem((DIM, HEADS * DIM), BF16), vmem((HEADS * DIM, 2 * TOK), BF16),
        vmem((DIM, 2 * TOK), BF16), vmem((SERVED, FEAT, FEAT), BF16), vmem((SERVED, FEAT, FEAT), BF16),
        vmem((SERVED, FEAT + HEAD, 2 * TOK), BF16), vmem((BANDS // 2, FEAT + HEAD, 2 * TOK), BF16),
        vmem((OWNERS, 8, FEAT), F32), vmem((FRAMES, 8, FEAT), F32), vmem((FRAMES, 8, FEAT), F32),
        vmem((8, FEAT), F32), vmem((FRAMES, 8, FEAT), F32), vmem((OWNERS, 8, FEAT), F32),
        vmem((BANDS, TAPS * CH, TOK), F32), vmem((BANDS, CH, TOK), BF16),
        vmem((BANDS, CH, TOK), BF16),
        dma((18,)), dma((9,)), pltpu.SemaphoreType.REGULAR((5,)), dma, dma, dma, dma, dma, dma, dma, dma, dma,
    ]
    return pl.pallas_call(
        kernel,
        out_shape=jax.ShapeDtypeStruct((1, 8, DIM), F32),
        in_specs=[pl.BlockSpec(memory_space=pltpu.HBM)] * 12,
        out_specs=pl.BlockSpec(memory_space=pltpu.VMEM),
        scratch_shapes=scratch,
        compiler_params=pltpu.CompilerParams(
            collective_id=0, has_side_effects=True, vmem_limit_bytes=63 * 1024 * 1024
        ),
        name="propagate",
    )(
        frames, labels, table, qkv, eo, gain.reshape(1, DIM), kp, vp, rp, decay,
        conv.transpose(0, 1, 3, 2).reshape(TAPS, CH, DIM), up.T,
    )


def solution(mesh):
    return jax.shard_map(
        shards,
        mesh=mesh,
        in_specs=(
            P("tm", "space", None, None), P("space", None), P(), P(), P(), P(), P(), P(), P(),
            P("tm", None), P(), P(),
        ),
        out_specs=P("tm", "space", None),
        check_vma=False,
    )
```

```python
import math

import jax
import jax.numpy as jnp
from jax import lax
from jax.experimental import pallas as pl
from jax.experimental.pallas import tpu as pltpu
from jax.sharding import PartitionSpec as P

MESH = pl.DeviceIdType.MESH
BF16 = jnp.bfloat16
F32 = jnp.float32

FRAMES = 64
BANDS = 8
OWNERS = 16
STRIDE = FRAMES // OWNERS
TOK = 128
DIM = 256
HEADS = 8
HEAD = DIM // HEADS
FEAT = 128
CH = 64
TAPS = 9
SERVED = 3
FAR_FIRST = (4, 3, 5, 2, 6, 1, 7)


def mm(a, b):
    return jnp.dot(a, b, preferred_element_type=F32)


def mm_nt(a, b):
    return lax.dot_general(a, b, (((1,), (1,)), ((), ())), preferred_element_type=F32)


def turned(x):
    return x.astype(F32).T.astype(x.dtype)


def iota(shape, dim):
    return lax.broadcasted_iota(jnp.int32, shape, dim)


def three_parts(x):
    high = x.astype(BF16)
    rest = x - high.astype(F32)
    middle = rest.astype(BF16)
    low = (rest - middle.astype(F32)).astype(BF16)
    return high, middle, low


def kernel(
    frames, labels, table, qkv, eo, gain, kp, vp, rp, decay, conv, up,
    out,
    x_v, lab_v, tab_v, qkv_v, eo_v, gain_v, kp_v, vp_v, rp_v, dec_v, conv_v, up_v,
    wq_t, eo_t, kp_t, vp_t, tab_t, gain_b, taps_t, up_x, spread,
    pool, hot, xt, kmask, v_mask, weights, e_tmp, state_out, state_part, ke_out, ke,
    state, states, decays, decay_own, memories, memory,
    conved, part, parts,
    load, send, greetings, pool_in, hot_in, xt_in, part_state_in, ke_in, decay_in, state_in, memory_in, part_in,
):
    tm, sp = lax.axis_index("tm"), lax.axis_index("space")
    is_owner = lax.rem(tm, STRIDE) == 0
    side, pair = lax.rem(sp, 2), sp // 2
    heads = [sp] + [lax.rem(sp + BANDS + (2 * side - 1) * k, BANDS) for k in range(1, SERVED + 1)]

    core, y, x = lax.rem(tm, 2), lax.rem(tm // 2, 8), tm // 16
    along_y = [x * 16 + lax.rem(y + k, 8) * 2 + core for k in (1, 7)]
    along_x = [lax.rem(x + k, 4) * 16 + y * 2 + core for k in (1, 3)]

    barrier = pltpu.get_barrier_semaphore()
    for k in range(1, BANDS):
        pl.semaphore_signal(
            barrier, inc=1, device_id=(tm, lax.rem(sp + k, BANDS)), device_id_type=MESH
        )

    partner = 1 - 2 * core
    for t in (*along_y, *along_x, *(t + partner for t in along_y), tm + partner):
        pl.semaphore_signal(barrier, inc=1, device_id=(t, sp), device_id_type=MESH)

    def greet(n):
        for t in along_y if n < 3 else along_x:
            pl.semaphore_signal(
                greetings.at[n], inc=1, device_id=(t, sp), device_id_type=MESH
            )

    def greeted(n):
        pl.semaphore_wait(greetings.at[n], 2)

    col = pl.multiple_of(sp * FEAT, FEAT)
    loads = [
        (frames.at[0], x_v),
        (labels, lab_v),
        (decay, dec_v),
        (qkv, qkv_v),
        (table, tab_v),
        (eo, eo_v),
        (gain, gain_v),
        (rp.at[pl.ds(col, FEAT), :], rp_v),
        (conv, conv_v),
        (up, up_v),
    ]
    for k, h in enumerate(heads):
        at = pl.ds(pl.multiple_of(h * FEAT, FEAT), FEAT)
        loads.append((kp.at[:, at], kp_v.at[k]))
        loads.append((vp.at[:, at], vp_v.at[k]))
    loads = [pltpu.make_async_copy(s, d, load.at[n]) for n, (s, d) in enumerate(loads)]
    for c in loads:
        c.start()

    loads[0].wait()
    own = x_v[...].reshape(TOK, DIM)
    pr, pc = iota((TOK // 4, TOK), 0), iota((TOK // 4, TOK), 1)
    quarter = jnp.where(lax.rem(pc, 64) // 2 == pr, 0.25, 0.0).astype(BF16)
    pool[sp] = mm(quarter, own).astype(BF16)
    loads[1].wait()
    lab = lab_v[...]
    lab_row = jnp.concatenate([lab[0:1], lab[1:2]], axis=1)
    hit = (jnp.broadcast_to(lab_row, (16, TOK)) == iota((16, TOK), 0)) & (tm == 0)
    hot[side] = jnp.where(hit, 1.0, 0.0).astype(BF16)
    loads[2].wait()
    rate = jnp.sum(
        jnp.where(iota((1, HEADS), 1) == sp, dec_v[...], 0.0), axis=1, keepdims=True
    )
    decay_own[...] = jnp.broadcast_to(rate, (8, FEAT))

    pl.semaphore_wait(barrier, BANDS - 1 + 7)

    def to_band(place, src, dst, n, sem):
        pltpu.make_async_remote_copy(
            src_ref=src,
            dst_ref=dst,
            send_sem=send.at[n],
            recv_sem=sem,
            device_id=(tm, place),
            device_id_type=MESH,
        ).start()

    def arrived(ref, sem):
        pltpu.make_async_copy(ref, ref, sem).wait()

    greet(0)
    for k in FAR_FIRST:
        to_band(lax.rem(sp + k, BANDS), pool.at[sp], pool.at[sp], 0, pool_in)
    xt[side] = own.astype(F32).T.astype(BF16)
    to_band(sp + 1 - 2 * side, xt.at[side], xt.at[side], 2, xt_in)
    to_band(sp + 1 - 2 * side, hot.at[side], hot.at[side], 1, hot_in)

    def to_owners(src, dst, n, sem):
        for c in range(OWNERS):
            @pl.when(tm != c * STRIDE)
            def _():
                pltpu.make_async_remote_copy(
                    src_ref=src(c),
                    dst_ref=dst.at[tm],
                    send_sem=send.at[n],
                    recv_sem=sem,
                    device_id=(c * STRIDE, sp),
                    device_id_type=MESH,
                ).start()

    for c in loads[3:]:
        c.wait()
    wq_t[...] = turned(qkv_v[:, :DIM])
    eo_t[...] = turned(eo_v[...])
    greeted(0)
    greet(1)
    for k in range(SERVED + 1):
        kp_t[k * FEAT : (k + 1) * FEAT, :] = turned(kp_v[k])
        vp_t[k * FEAT : (k + 1) * FEAT, :] = turned(vp_v[k])
    greeted(1)
    greet(2)
    tab = jnp.concatenate([tab_v[...], jnp.zeros((12, DIM), F32)], axis=0)
    tab_t[...] = turned(jnp.concatenate(three_parts(tab), axis=0))
    gain_b[...] = jnp.broadcast_to(gain_v[...], (TOK, DIM)).T

    arrived(pool.at[pl.ds(0, BANDS - 1)], pool_in)
    pooled = pool[...].reshape(BANDS * TOK // 4, DIM)
    kv = mm(pooled, qkv_v[:, DIM:])
    keys = kv[:, :DIM].astype(BF16)
    values = kv[:, DIM:].T.astype(BF16)
    lane_head, row_head = iota((DIM, DIM), 1) // HEAD, iota((DIM, DIM), 0) // HEAD
    for h in range(HEADS):
        kmask[h * DIM : (h + 1) * DIM, :] = jnp.where(lane_head == h, keys, jnp.zeros_like(keys))
        v_mask[:, h * DIM : (h + 1) * DIM] = jnp.where(row_head == h, values, jnp.zeros_like(values))

    greeted(2)
    greet(3)

    factor = HEAD**-0.5 * math.log2(math.e)
    arrived(xt.at[0], xt_in)
    arrived(hot.at[0], hot_in)
    xp = jnp.concatenate([xt[0], xt[1]], axis=1)
    q = mm(wq_t[...], xp).astype(BF16)
    scores = mm(kmask[...], q)
    inverse = []
    for h in range(HEADS):
        s = scores[h * DIM : (h + 1) * DIM]
        w = jnp.exp2((s - jnp.max(s, axis=0, keepdims=True)) * factor)
        inverse.append(
            jnp.broadcast_to(1.0 / jnp.sum(w, axis=0, keepdims=True), (HEAD, 2 * TOK))
        )
        weights[h * DIM : (h + 1) * DIM, :] = w.astype(BF16)
    summed = mm(v_mask[...], weights[...])
    attended = (summed * jnp.concatenate(inverse, axis=0)).astype(BF16)
    greeted(3)
    greet(4)
    hidden = xp.astype(F32) + mm(eo_t[...], attended)
    scale = lax.rsqrt(jnp.mean(hidden * hidden, axis=0, keepdims=True) + 1e-06)
    gains = jnp.concatenate([gain_b[...], gain_b[...]], axis=1)
    encoded = (hidden * scale * gains).astype(BF16)
    e_tmp[...] = encoded
    mark = jnp.concatenate([hot[0], hot[1]], axis=1)
    mark = jnp.concatenate([mark, mark, mark], axis=0)
    told = (encoded.astype(F32) + mm(tab_t[...], mark)).astype(BF16)
    keys = mm(kp_t[...], encoded).astype(BF16)
    values = mm(vp_t[...], told).astype(BF16)

    def share(k):
        at = slice(k * FEAT, (k + 1) * FEAT)
        return mm_nt(values[at], keys[at]) * (BANDS * TOK) ** -0.5

    for k in range(SERVED, 0, -1):
        state_out[k - 1] = share(k).astype(BF16)
        to_band(heads[k], state_out.at[k - 1], state_part.at[k - 1], 7, part_state_in)
    total = share(0)
    for k in range(SERVED + 1):
        h = pl.multiple_of(heads[k] * HEAD, HEAD)
        both = jnp.concatenate([keys[k * FEAT : (k + 1) * FEAT], e_tmp[pl.ds(h, HEAD), :]], axis=0)
        if k == 0:
            ke[pair] = both
        else:
            ke_out[k - 1] = both
            to_band(heads[k], ke_out.at[k - 1], ke.at[pair], 8, ke_in)
    greeted(4)
    to_owners(lambda c: decay_own, decays, 3, decay_in)

    here = jnp.where(iota((DIM, HEAD), 0) == sp * HEAD + iota((DIM, HEAD), 1), 1.0, 0.0).astype(BF16)

    @pl.loop(0, TAPS)
    def _(n):
        both = mm_nt(conv_v[n], rp_v[...]).astype(BF16)
        own = mm(conv_v[n], here).astype(BF16)
        taps_t[pl.ds(pl.multiple_of(n * CH, CH), CH), :] = jnp.concatenate([both, own], axis=1)

    row, src_row = iota((32, 16), 0), iota((32, 16), 1)
    picks = jnp.where(src_row == 4 * lax.rem(row, 4) + row // 8, 1.0, 0.0).astype(BF16)
    up_x[...] = mm(picks, up_v[...]).astype(BF16)
    er, ec = iota((4 * TOK, DIM), 0), iota((4 * TOK, DIM), 1)
    spread[...] = jnp.where(ec == 4 * lax.rem(er, 64) + er // TOK, 1.0, 0.0).astype(BF16)

    arrived(state_part, part_state_in)
    for k in range(SERVED):
        total = total + state_part[k].astype(F32)
    state[...] = total.reshape(OWNERS, 8, FEAT)

    to_owners(lambda c: state.at[c], states, 4, state_in)

    @pl.when(is_owner)
    def _():
        states[tm] = state[tm // STRIDE]
        decays[tm] = decay_own[...]
        arrived(decays.at[pl.ds(0, FRAMES - 1)], decay_in)
        arrived(states.at[pl.ds(0, FRAMES - 1)], state_in)
        place = tm // STRIDE

        def frame(t, held):
            held = decays[t] * held
            memories[t] = held

            @pl.when(t != tm)
            def _():
                pltpu.make_async_remote_copy(
                    src_ref=memories.at[t],
                    dst_ref=memory.at[place],
                    send_sem=send.at[5],
                    recv_sem=memory_in,
                    device_id=(t, sp),
                    device_id_type=MESH,
                ).start()

            return held + states[t]

        lax.fori_loop(0, FRAMES, frame, jnp.zeros((8, FEAT), F32))
        memory[place] = memories[tm]
        arrived(memory.at[pl.ds(0, OWNERS - 1)], memory_in)

    @pl.when(jnp.logical_not(is_owner))
    def _():
        arrived(memory, memory_in)

    now = memory[...].reshape(FEAT, FEAT).astype(BF16)
    arrived(ke_out, ke_in)
    for p in range(BANDS // 2):
        read = (mm(now, ke[p, :FEAT, :]) * FEAT**-0.5).astype(BF16)
        c = mm(taps_t[...], jnp.concatenate([read, ke[p, FEAT:, :]], axis=0))
        conved[2 * p] = c[:, :TOK]
        conved[2 * p + 1] = c[:, TOK:]
    lane = iota((CH, TOK), 1)
    column = lax.rem(lane, 64)

    def tap(n, a, b):
        at = (a * 3 + b) * CH
        return conved[n, at : at + CH, :]

    for n in range(BANDS):
        shifted = []
        for b in range(3):
            late, early = tap(n, 2, b), tap(n, 0, b)
            if n > 0:
                late = late + tap(n - 1, 0, b)
            if n < BANDS - 1:
                early = early + tap(n + 1, 2, b)
            shifted.append(tap(n, 1, b) + pltpu.roll(jnp.where(lane >= 64, late, early), 64, 1))
        total = shifted[1]
        total = total + jnp.where(column != 63, pltpu.roll(shifted[2], TOK - 1, 1), 0.0)
        total = total + jnp.where(column != 0, pltpu.roll(shifted[0], 1, 1), 0.0)
        part[n] = total.astype(BF16)

        @pl.when(sp != n)
        def _():
            pltpu.make_async_remote_copy(
                src_ref=part.at[n],
                dst_ref=parts.at[sp],
                send_sem=send.at[6],
                recv_sem=part_in,
                device_id=(tm, n),
                device_id_type=MESH,
            ).start()

    parts[sp] = part[sp]
    arrived(parts.at[pl.ds(0, BANDS - 1)], part_in)
    total = parts[0].astype(F32)
    for n in range(1, BANDS):
        total = total + parts[n].astype(F32)
    cubic = total + 0.044715 * (total * total * total)
    hidden = (0.5 * total * (1.0 + jnp.tanh(math.sqrt(2 / math.pi) * cubic))).astype(BF16)
    pixels = mm(up_x[...], hidden)
    keep = (lax.rem(iota((32, TOK), 0) // 4, 2)) == (iota((32, TOK), 1) // 64)
    pixels = jnp.where(keep, pixels, 0.0)
    wide = jnp.concatenate([pixels[8 * b : 8 * b + 8] for b in range(4)], axis=1)
    high, middle, low = three_parts(wide)
    high = mm(high, spread[...])
    out[0] = high + (mm(middle, spread[...]) + mm(low, spread[...]))

    arrived(pool.at[pl.ds(0, BANDS - 1)], send.at[0])
    arrived(hot.at[0], send.at[1])
    arrived(xt.at[0], send.at[2])
    arrived(state_out, send.at[7])
    arrived(ke_out, send.at[8])

    @pl.when(is_owner)
    def _():
        arrived(state.at[pl.ds(0, OWNERS - 1)], send.at[3])
        arrived(state.at[pl.ds(0, OWNERS - 1)], send.at[4])
        arrived(memories.at[pl.ds(0, FRAMES - 1)], send.at[5])

    @pl.when(jnp.logical_not(is_owner))
    def _():
        arrived(state, send.at[3])
        arrived(state, send.at[4])

    arrived(part.at[pl.ds(0, BANDS - 1)], send.at[6])


def shards(frames, labels, table, qkv, eo, gain, kp, vp, rp, decay, conv, up):
    vmem = pltpu.VMEM
    dma = pltpu.SemaphoreType.DMA
    scratch = [
        vmem((2, 64, DIM), BF16), vmem((2, 64), jnp.int32), vmem((4, DIM), F32),
        vmem((DIM, 3 * DIM), BF16), vmem((DIM, DIM), BF16), vmem((1, DIM), F32),
        vmem((SERVED + 1, DIM, FEAT), BF16), vmem((SERVED + 1, DIM, FEAT), BF16), vmem((FEAT, DIM), BF16),
        vmem((1, HEADS), F32), vmem((TAPS, CH, DIM), BF16), vmem((16, CH), BF16),
        vmem((DIM, DIM), BF16), vmem((DIM, DIM), BF16), vmem(((SERVED + 1) * FEAT, DIM), BF16),
        vmem(((SERVED + 1) * FEAT, DIM), BF16), vmem((DIM, 48), BF16), vmem((DIM, TOK), F32),
        vmem((TAPS * CH, FEAT + HEAD), BF16), vmem((32, CH), BF16), vmem((4 * TOK, DIM), BF16),
        vmem((BANDS, TOK // 4, DIM), BF16), vmem((2, 16, TOK), BF16),
        vmem((2, DIM, TOK), BF16), vmem((HEADS * DIM, DIM), BF16),
        vmem((DIM, HEADS * DIM), BF16), vmem((HEADS * DIM, 2 * TOK), BF16),
        vmem((DIM, 2 * TOK), BF16), vmem((SERVED, FEAT, FEAT), BF16), vmem((SERVED, FEAT, FEAT), BF16),
        vmem((SERVED, FEAT + HEAD, 2 * TOK), BF16), vmem((BANDS // 2, FEAT + HEAD, 2 * TOK), BF16),
        vmem((OWNERS, 8, FEAT), F32), vmem((FRAMES, 8, FEAT), F32), vmem((FRAMES, 8, FEAT), F32),
        vmem((8, FEAT), F32), vmem((FRAMES, 8, FEAT), F32), vmem((OWNERS, 8, FEAT), F32),
        vmem((BANDS, TAPS * CH, TOK), F32), vmem((BANDS, CH, TOK), BF16),
        vmem((BANDS, CH, TOK), BF16),
        dma((18,)), dma((9,)), pltpu.SemaphoreType.REGULAR((5,)), dma, dma, dma, dma, dma, dma, dma, dma, dma,
    ]
    return pl.pallas_call(
        kernel,
        out_shape=jax.ShapeDtypeStruct((1, 8, DIM), F32),
        in_specs=[pl.BlockSpec(memory_space=pltpu.HBM)] * 12,
        out_specs=pl.BlockSpec(memory_space=pltpu.VMEM),
        scratch_shapes=scratch,
        compiler_params=pltpu.CompilerParams(
            collective_id=0, has_side_effects=True, vmem_limit_bytes=63 * 1024 * 1024
        ),
        name="propagate",
    )(
        frames, labels, table, qkv, eo, gain.reshape(1, DIM), kp, vp, rp, decay,
        conv.transpose(0, 1, 3, 2).reshape(TAPS, CH, DIM), up.T,
    )


def solution(mesh):
    return jax.shard_map(
        shards,
        mesh=mesh,
        in_specs=(
            P("tm", "space", None, None), P("space", None), P(), P(), P(), P(), P(), P(), P(),
            P("tm", None), P(), P(),
        ),
        out_specs=P("tm", "space", None),
        check_vma=False,
    )
```

```python
import math

import jax
import jax.numpy as jnp
from jax import lax
from jax.experimental import pallas as pl
from jax.experimental.pallas import tpu as pltpu
from jax.sharding import PartitionSpec as P

MESH = pl.DeviceIdType.MESH
BF16 = jnp.bfloat16
F32 = jnp.float32

FRAMES = 64
BANDS = 8
OWNERS = 16
STRIDE = FRAMES // OWNERS
TOK = 128
DIM = 256
HEADS = 8
HEAD = DIM // HEADS
FEAT = 128
CH = 64
TAPS = 9
SERVED = 3
FAR_FIRST = (4, 3, 5, 2, 6, 1, 7)


def mm(a, b):
    return jnp.dot(a, b, preferred_element_type=F32)


def mm_nt(a, b):
    return lax.dot_general(a, b, (((1,), (1,)), ((), ())), preferred_element_type=F32)


def turned(x):
    return x.astype(F32).T.astype(x.dtype)


def iota(shape, dim):
    return lax.broadcasted_iota(jnp.int32, shape, dim)


def three_parts(x):
    high = x.astype(BF16)
    rest = x - high.astype(F32)
    middle = rest.astype(BF16)
    low = (rest - middle.astype(F32)).astype(BF16)
    return high, middle, low


def kernel(
    frames, labels, table, qkv, eo, gain, kp, vp, rp, decay, conv, up,
    out,
    x_v, lab_v, tab_v, qkv_v, eo_v, gain_v, kp_v, vp_v, rp_v, dec_v, conv_v, up_v,
    wq_t, eo_t, kp_t, vp_t, tab_t, gain_b, taps_t, up_x, spread,
    pool, hot, xt, kmask, v_mask, weights, e_tmp, state_out, state_part, ke_out, ke,
    state, states, decays, decay_own, memories, memory,
    conved, part, parts,
    load, send, greetings, pool_in, hot_in, xt_in, part_state_in, ke_in, decay_in, state_in, memory_in, part_in,
):
    tm, sp = lax.axis_index("tm"), lax.axis_index("space")
    is_owner = lax.rem(tm, STRIDE) == 0
    side, pair = lax.rem(sp, 2), sp // 2
    heads = [sp] + [lax.rem(sp + BANDS + (2 * side - 1) * k, BANDS) for k in range(1, SERVED + 1)]

    core, y, x = lax.rem(tm, 2), lax.rem(tm // 2, 8), tm // 16
    along_y = [x * 16 + lax.rem(y + k, 8) * 2 + core for k in (1, 7)]
    along_x = [lax.rem(x + k, 4) * 16 + y * 2 + core for k in (1, 3)]

    barrier = pltpu.get_barrier_semaphore()
    for k in range(1, BANDS):
        pl.semaphore_signal(
            barrier, inc=1, device_id=(tm, lax.rem(sp + k, BANDS)), device_id_type=MESH
        )

    partner = 1 - 2 * core
    for t in (*along_y, *along_x, *(t + partner for t in along_y), tm + partner):
        pl.semaphore_signal(barrier, inc=1, device_id=(t, sp), device_id_type=MESH)

    def greet(n):
        for t in along_y if n < 3 else along_x:
            pl.semaphore_signal(
                greetings.at[n], inc=1, device_id=(t, sp), device_id_type=MESH
            )

    def greeted(n):
        pl.semaphore_wait(greetings.at[n], 2)

    col = pl.multiple_of(sp * FEAT, FEAT)
    loads = [
        (frames.at[0], x_v),
        (labels, lab_v),
        (decay, dec_v),
        (qkv, qkv_v),
        (table, tab_v),
        (eo, eo_v),
        (gain, gain_v),
        (rp.at[pl.ds(col, FEAT), :], rp_v),
        (conv, conv_v),
        (up, up_v),
    ]
    for k, h in enumerate(heads):
        at = pl.ds(pl.multiple_of(h * FEAT, FEAT), FEAT)
        loads.append((kp.at[:, at], kp_v.at[k]))
        loads.append((vp.at[:, at], vp_v.at[k]))
    loads = [pltpu.make_async_copy(s, d, load.at[n]) for n, (s, d) in enumerate(loads)]
    for c in loads:
        c.start()

    loads[0].wait()
    own = x_v[...].reshape(TOK, DIM)
    pr, pc = iota((TOK // 4, TOK), 0), iota((TOK // 4, TOK), 1)
    quarter = jnp.where(lax.rem(pc, 64) // 2 == pr, 0.25, 0.0).astype(BF16)
    pool[sp] = mm(quarter, own).astype(BF16)
    loads[1].wait()
    lab = lab_v[...]
    lab_row = jnp.concatenate([lab[0:1], lab[1:2]], axis=1)
    hit = (jnp.broadcast_to(lab_row, (16, TOK)) == iota((16, TOK), 0)) & (tm == 0)
    hot[side] = jnp.where(hit, 1.0, 0.0).astype(BF16)
    loads[2].wait()
    rate = jnp.sum(
        jnp.where(iota((1, HEADS), 1) == sp, dec_v[...], 0.0), axis=1, keepdims=True
    )
    decay_own[...] = jnp.broadcast_to(rate, (8, FEAT))

    pl.semaphore_wait(barrier, BANDS - 1 + 7)

    def to_band(place, src, dst, n, sem):
        pltpu.make_async_remote_copy(
            src_ref=src,
            dst_ref=dst,
            send_sem=send.at[n],
            recv_sem=sem,
            device_id=(tm, place),
            device_id_type=MESH,
        ).start()

    def arrived(ref, sem):
        pltpu.make_async_copy(ref, ref, sem).wait()

    greet(0)
    for k in FAR_FIRST:
        to_band(lax.rem(sp + k, BANDS), pool.at[sp], pool.at[sp], 0, pool_in)
    xt[side] = own.astype(F32).T.astype(BF16)
    to_band(sp + 1 - 2 * side, xt.at[side], xt.at[side], 2, xt_in)
    to_band(sp + 1 - 2 * side, hot.at[side], hot.at[side], 1, hot_in)

    def to_owners(src, dst, n, sem):
        for c in range(OWNERS):
            @pl.when(tm != c * STRIDE)
            def _():
                pltpu.make_async_remote_copy(
                    src_ref=src(c),
                    dst_ref=dst.at[tm],
                    send_sem=send.at[n],
                    recv_sem=sem,
                    device_id=(c * STRIDE, sp),
                    device_id_type=MESH,
                ).start()

    for c in loads[3:]:
        c.wait()
    wq_t[...] = turned(qkv_v[:, :DIM])
    eo_t[...] = turned(eo_v[...])
    greeted(0)
    greet(1)
    for k in range(SERVED + 1):
        kp_t[k * FEAT : (k + 1) * FEAT, :] = turned(kp_v[k])
        vp_t[k * FEAT : (k + 1) * FEAT, :] = turned(vp_v[k])
    greeted(1)
    greet(2)
    tab = jnp.concatenate([tab_v[...], jnp.zeros((12, DIM), F32)], axis=0)
    tab_t[...] = turned(jnp.concatenate(three_parts(tab), axis=0))
    gain_b[...] = jnp.broadcast_to(gain_v[...], (TOK, DIM)).T

    arrived(pool.at[pl.ds(0, BANDS - 1)], pool_in)
    pooled = pool[...].reshape(BANDS * TOK // 4, DIM)
    kv = mm(pooled, qkv_v[:, DIM:])
    keys = kv[:, :DIM].astype(BF16)
    values = kv[:, DIM:].T.astype(BF16)
    lane_head, row_head = iota((DIM, DIM), 1) // HEAD, iota((DIM, DIM), 0) // HEAD
    for h in range(HEADS):
        kmask[h * DIM : (h + 1) * DIM, :] = jnp.where(lane_head == h, keys, jnp.zeros_like(keys))
        v_mask[:, h * DIM : (h + 1) * DIM] = jnp.where(row_head == h, values, jnp.zeros_like(values))

    greeted(2)
    greet(3)

    factor = HEAD**-0.5 * math.log2(math.e)
    arrived(xt.at[0], xt_in)
    arrived(hot.at[0], hot_in)
    xp = jnp.concatenate([xt[0], xt[1]], axis=1)
    q = mm(wq_t[...], xp).astype(BF16)
    scores = mm(kmask[...], q)
    inverse = []
    for h in range(HEADS):
        s = scores[h * DIM : (h + 1) * DIM]
        w = jnp.exp2((s - jnp.max(s, axis=0, keepdims=True)) * factor)
        inverse.append(
            jnp.broadcast_to(1.0 / jnp.sum(w, axis=0, keepdims=True), (HEAD, 2 * TOK))
        )
        weights[h * DIM : (h + 1) * DIM, :] = w.astype(BF16)
    summed = mm(v_mask[...], weights[...])
    attended = (summed * jnp.concatenate(inverse, axis=0)).astype(BF16)
    greeted(3)
    greet(4)
    hidden = xp.astype(F32) + mm(eo_t[...], attended)
    scale = lax.rsqrt(jnp.mean(hidden * hidden, axis=0, keepdims=True) + 1e-06)
    gains = jnp.concatenate([gain_b[...], gain_b[...]], axis=1)
    encoded = (hidden * scale * gains).astype(BF16)
    e_tmp[...] = encoded
    mark = jnp.concatenate([hot[0], hot[1]], axis=1)
    mark = jnp.concatenate([mark, mark, mark], axis=0)
    told = (encoded.astype(F32) + mm(tab_t[...], mark)).astype(BF16)
    keys = mm(kp_t[...], encoded).astype(BF16)
    values = mm(vp_t[...], told).astype(BF16)

    def share(k):
        at = slice(k * FEAT, (k + 1) * FEAT)
        return mm_nt(values[at], keys[at]) * (BANDS * TOK) ** -0.5

    for k in range(SERVED, 0, -1):
        state_out[k - 1] = share(k).astype(BF16)
        to_band(heads[k], state_out.at[k - 1], state_part.at[k - 1], 7, part_state_in)
    total = share(0)
    for k in range(SERVED + 1):
        h = pl.multiple_of(heads[k] * HEAD, HEAD)
        both = jnp.concatenate([keys[k * FEAT : (k + 1) * FEAT], e_tmp[pl.ds(h, HEAD), :]], axis=0)
        if k == 0:
            ke[pair] = both
        else:
            ke_out[k - 1] = both
            to_band(heads[k], ke_out.at[k - 1], ke.at[pair], 8, ke_in)
    greeted(4)
    to_owners(lambda c: decay_own, decays, 3, decay_in)

    here = jnp.where(iota((DIM, HEAD), 0) == sp * HEAD + iota((DIM, HEAD), 1), 1.0, 0.0).astype(BF16)

    @pl.loop(0, TAPS)
    def _(n):
        both = mm_nt(conv_v[n], rp_v[...]).astype(BF16)
        own = mm(conv_v[n], here).astype(BF16)
        taps_t[pl.ds(pl.multiple_of(n * CH, CH), CH), :] = jnp.concatenate([both, own], axis=1)

    row, src_row = iota((32, 16), 0), iota((32, 16), 1)
    picks = jnp.where(src_row == 4 * lax.rem(row, 4) + row // 8, 1.0, 0.0).astype(BF16)
    up_x[...] = mm(picks, up_v[...]).astype(BF16)
    er, ec = iota((4 * TOK, DIM), 0), iota((4 * TOK, DIM), 1)
    spread[...] = jnp.where(ec == 4 * lax.rem(er, 64) + er // TOK, 1.0, 0.0).astype(BF16)

    arrived(state_part, part_state_in)
    for k in range(SERVED):
        total = total + state_part[k].astype(F32)
    state[...] = total.reshape(OWNERS, 8, FEAT)

    to_owners(lambda c: state.at[c], states, 4, state_in.at[x])

    @pl.when(is_owner)
    def _():
        states[tm] = state[tm // STRIDE]
        decays[tm] = decay_own[...]
        arrived(decays.at[pl.ds(0, FRAMES - 1)], decay_in)
        place = tm // STRIDE

        def frame(t, held):
            held = decays[t] * held
            memories[t] = held

            @pl.when(t != tm)
            def _():
                pltpu.make_async_remote_copy(
                    src_ref=memories.at[t],
                    dst_ref=memory.at[place],
                    send_sem=send.at[5],
                    recv_sem=memory_in,
                    device_id=(t, sp),
                    device_id_type=MESH,
                ).start()

            return held + states[t]

        held = jnp.zeros((8, FEAT), F32)
        for g in range(4):
            @pl.when(x == g)
            def _():
                arrived(states.at[pl.ds(0, FRAMES // 4 - 1)], state_in.at[g])

            @pl.when(x != g)
            def _():
                arrived(states.at[pl.ds(0, FRAMES // 4)], state_in.at[g])

            held = lax.fori_loop(g * FRAMES // 4, (g + 1) * FRAMES // 4, frame, held)
        memory[place] = memories[tm]
        arrived(memory.at[pl.ds(0, OWNERS - 1)], memory_in)

    @pl.when(jnp.logical_not(is_owner))
    def _():
        arrived(memory, memory_in)

    now = memory[...].reshape(FEAT, FEAT).astype(BF16)
    arrived(ke_out, ke_in)
    for p in range(BANDS // 2):
        read = (mm(now, ke[p, :FEAT, :]) * FEAT**-0.5).astype(BF16)
        c = mm(taps_t[...], jnp.concatenate([read, ke[p, FEAT:, :]], axis=0))
        conved[2 * p] = c[:, :TOK]
        conved[2 * p + 1] = c[:, TOK:]
    lane = iota((CH, TOK), 1)
    column = lax.rem(lane, 64)

    def tap(n, a, b):
        at = (a * 3 + b) * CH
        return conved[n, at : at + CH, :]

    for n in range(BANDS):
        shifted = []
        for b in range(3):
            late, early = tap(n, 2, b), tap(n, 0, b)
            if n > 0:
                late = late + tap(n - 1, 0, b)
            if n < BANDS - 1:
                early = early + tap(n + 1, 2, b)
            shifted.append(tap(n, 1, b) + pltpu.roll(jnp.where(lane >= 64, late, early), 64, 1))
        total = shifted[1]
        total = total + jnp.where(column != 63, pltpu.roll(shifted[2], TOK - 1, 1), 0.0)
        total = total + jnp.where(column != 0, pltpu.roll(shifted[0], 1, 1), 0.0)
        part[n] = total.astype(BF16)

        @pl.when(sp != n)
        def _():
            pltpu.make_async_remote_copy(
                src_ref=part.at[n],
                dst_ref=parts.at[sp],
                send_sem=send.at[6],
                recv_sem=part_in,
                device_id=(tm, n),
                device_id_type=MESH,
            ).start()

    parts[sp] = part[sp]
    arrived(parts.at[pl.ds(0, BANDS - 1)], part_in)
    total = parts[0].astype(F32)
    for n in range(1, BANDS):
        total = total + parts[n].astype(F32)
    cubic = total + 0.044715 * (total * total * total)
    hidden = (0.5 * total * (1.0 + jnp.tanh(math.sqrt(2 / math.pi) * cubic))).astype(BF16)
    pixels = mm(up_x[...], hidden)
    keep = (lax.rem(iota((32, TOK), 0) // 4, 2)) == (iota((32, TOK), 1) // 64)
    pixels = jnp.where(keep, pixels, 0.0)
    wide = jnp.concatenate([pixels[8 * b : 8 * b + 8] for b in range(4)], axis=1)
    high, middle, low = three_parts(wide)
    high = mm(high, spread[...])
    out[0] = high + (mm(middle, spread[...]) + mm(low, spread[...]))

    arrived(pool.at[pl.ds(0, BANDS - 1)], send.at[0])
    arrived(hot.at[0], send.at[1])
    arrived(xt.at[0], send.at[2])
    arrived(state_out, send.at[7])
    arrived(ke_out, send.at[8])

    @pl.when(is_owner)
    def _():
        arrived(state.at[pl.ds(0, OWNERS - 1)], send.at[3])
        arrived(state.at[pl.ds(0, OWNERS - 1)], send.at[4])
        arrived(memories.at[pl.ds(0, FRAMES - 1)], send.at[5])

    @pl.when(jnp.logical_not(is_owner))
    def _():
        arrived(state, send.at[3])
        arrived(state, send.at[4])

    arrived(part.at[pl.ds(0, BANDS - 1)], send.at[6])


def shards(frames, labels, table, qkv, eo, gain, kp, vp, rp, decay, conv, up):
    vmem = pltpu.VMEM
    dma = pltpu.SemaphoreType.DMA
    scratch = [
        vmem((2, 64, DIM), BF16), vmem((2, 64), jnp.int32), vmem((4, DIM), F32),
        vmem((DIM, 3 * DIM), BF16), vmem((DIM, DIM), BF16), vmem((1, DIM), F32),
        vmem((SERVED + 1, DIM, FEAT), BF16), vmem((SERVED + 1, DIM, FEAT), BF16), vmem((FEAT, DIM), BF16),
        vmem((1, HEADS), F32), vmem((TAPS, CH, DIM), BF16), vmem((16, CH), BF16),
        vmem((DIM, DIM), BF16), vmem((DIM, DIM), BF16), vmem(((SERVED + 1) * FEAT, DIM), BF16),
        vmem(((SERVED + 1) * FEAT, DIM), BF16), vmem((DIM, 48), BF16), vmem((DIM, TOK), F32),
        vmem((TAPS * CH, FEAT + HEAD), BF16), vmem((32, CH), BF16), vmem((4 * TOK, DIM), BF16),
        vmem((BANDS, TOK // 4, DIM), BF16), vmem((2, 16, TOK), BF16),
        vmem((2, DIM, TOK), BF16), vmem((HEADS * DIM, DIM), BF16),
        vmem((DIM, HEADS * DIM), BF16), vmem((HEADS * DIM, 2 * TOK), BF16),
        vmem((DIM, 2 * TOK), BF16), vmem((SERVED, FEAT, FEAT), BF16), vmem((SERVED, FEAT, FEAT), BF16),
        vmem((SERVED, FEAT + HEAD, 2 * TOK), BF16), vmem((BANDS // 2, FEAT + HEAD, 2 * TOK), BF16),
        vmem((OWNERS, 8, FEAT), F32), vmem((FRAMES, 8, FEAT), F32), vmem((FRAMES, 8, FEAT), F32),
        vmem((8, FEAT), F32), vmem((FRAMES, 8, FEAT), F32), vmem((OWNERS, 8, FEAT), F32),
        vmem((BANDS, TAPS * CH, TOK), F32), vmem((BANDS, CH, TOK), BF16),
        vmem((BANDS, CH, TOK), BF16),
        dma((18,)), dma((9,)), pltpu.SemaphoreType.REGULAR((5,)), dma, dma, dma, dma, dma, dma, dma((4,)), dma, dma,
    ]
    return pl.pallas_call(
        kernel,
        out_shape=jax.ShapeDtypeStruct((1, 8, DIM), F32),
        in_specs=[pl.BlockSpec(memory_space=pltpu.HBM)] * 12,
        out_specs=pl.BlockSpec(memory_space=pltpu.VMEM),
        scratch_shapes=scratch,
        compiler_params=pltpu.CompilerParams(
            collective_id=0, has_side_effects=True, vmem_limit_bytes=63 * 1024 * 1024
        ),
        name="propagate",
    )(
        frames, labels, table, qkv, eo, gain.reshape(1, DIM), kp, vp, rp, decay,
        conv.transpose(0, 1, 3, 2).reshape(TAPS, CH, DIM), up.T,
    )


def solution(mesh):
    return jax.shard_map(
        shards,
        mesh=mesh,
        in_specs=(
            P("tm", "space", None, None), P("space", None), P(), P(), P(), P(), P(), P(), P(),
            P("tm", None), P(), P(),
        ),
        out_specs=P("tm", "space", None),
        check_vma=False,
    )
```
